512 devices in a mesh: section: 32 (over y_lo, x, core), dp: 16 (over y_hi, z).
Axes of the slice: x: 4, y: 8 (y_hi: 2, y_lo: 4; y = y_hi * 4 + y_lo), z: 8, core: 2. Of those that a mesh axis runs over, the one named last changes fastest.
Arguments:
- down_in: bfloat16 [32, 512, 8192], P('section', None, 'dp'), may hold values from -8 to 8
- up_in: bfloat16 [32, 512, 8192], P('section', None, 'dp'), may hold values from -8 to 8
- down_cot: bfloat16 [32, 512, 8192], P('section', None, 'dp'), may hold values from -0.03125 to 0.03125
- up_cot: bfloat16 [32, 512, 8192], P('section', None, 'dp'), may hold values from -0.03125 to 0.03125
- adapt_a: bfloat16 [32, 8192, 32], P('section', 'dp'), may hold values from -0.0625 to 0.0625
- adapt_b: bfloat16 [32, 32, 8192], P('section', None, 'dp'), may hold values from -1 to 1
- head_gain: float32 [4, 8192], replicated, may hold values from 0.5 to 1.5
- cand: bfloat16 [32, 8192], replicated, may hold values from -3 to 3
- down_ids: int32 [512], replicated, may hold values from 0 to 31
- up_ids: int32 [512], replicated, may hold values from 0 to 31
- offsets: int32 [4], replicated, may hold values from 1 to 4
- loss_weights: int32 [4], replicated, may hold values from 1 to 4
Outputs:
- down_next: bfloat16 [32, 512, 8192], P('section', None, 'dp')
- up_next: bfloat16 [32, 512, 8192], P('section', None, 'dp')
- down_back: bfloat16 [32, 512, 8192], P('section', None, 'dp')
- up_back: bfloat16 [32, 512, 8192], P('section', None, 'dp')
- grad_a: float32 [32, 8192, 32], P('section', 'dp')
- grad_b: float32 [32, 32, 8192], P('section', None, 'dp')
- loss: float32 [1], replicated
The draws below stay inside these ranges and needn't reach their ends.
All inputs are finite; a program needn't handle non-finite values.
Results may differ from the reference program's by a relative error of at most 0.005.
Values may be sent and summed in bfloat16 or wider, within the bound.
No kernel may reach another device: no remote copies, remote signals or barrier semaphores. Data moves between devices by JAX's collectives and lax.ppermute only.
A program may use at most 64 MiB of HBM per device.

```python
import jax
import jax.numpy as jnp
from jax import lax

D = 8192
R = 32
M = 32
K = 4
CAND = 32
S = 32
TOKENS = 512
N_DP = 16


def leading_sign(key):
    shared = jax.random.normal(jax.random.fold_in(key, 11), (D,), jnp.float32)
    return jnp.where(shared >= 0.0, 1.0, -1.0)


def draw_down_in(key, part):
    sign_row = leading_sign(key)
    key = jax.random.fold_in(key, 3)
    values = jax.random.truncated_normal(key, -6.0, 6.0, (S, TOKENS, D), jnp.float32) + 0.5 * sign_row[None, None, :]
    return values.astype(jnp.bfloat16)


def draw_up_in(key, part):
    sign_row = leading_sign(key)
    key = jax.random.fold_in(key, 4)
    values = jax.random.truncated_normal(key, -6.0, 6.0, (S, TOKENS, D), jnp.float32) + 0.5 * sign_row[None, None, :]
    return values.astype(jnp.bfloat16)


def draw_cand(key, part):
    sign_row = leading_sign(key)
    key = jax.random.fold_in(key, 5)
    scale_unit = 3.0 / D ** 0.5
    other_key = jax.random.fold_in(key, 2)
    noise_rows = jax.random.truncated_normal(other_key, -6.0, 6.0, (CAND - 1, D), jnp.float32)
    lead_row = sign_row * (6.0 / D ** 0.5)
    values = jnp.concatenate([lead_row[None], noise_rows], axis=0)
    return (values * scale_unit).astype(jnp.bfloat16)


def set_ends(values, key, smallest, top_value):
    longest = values.shape.index(max(values.shape))
    spots = []
    for shift in (0, 1):
        where = [jax.random.randint(jax.random.fold_in(key, axis), (), 0, length) for axis, length in enumerate(values.shape)]
        where[longest] = (where[longest] + shift) % values.shape[longest]
        spots.append(tuple(where))
    return values.at[spots[0]].set(smallest).at[spots[1]].set(top_value)


def steps_of(key, extent, shards, smallest, largest):
    factor_of = 1.0
    for axis_at, shards_of in shards:
        draws = jax.random.uniform(jax.random.fold_in(jax.random.fold_in(key, 6), axis_at), (shards_of,), jnp.float32, smallest / len(shards), largest / len(shards))
        factor_of = factor_of * jnp.repeat(jnp.exp(draws), extent[axis_at] // shards_of).reshape((-1,) + (1,) * (len(extent) - 1 - axis_at))
    return factor_of


def normal_values(stream_key, dims, scale, reach, cuts=(), held_as=jnp.bfloat16):
    drawn = jax.random.normal(stream_key, dims, jnp.float32) * scale
    if len(cuts) > 0:
        drawn = steps_of(stream_key, dims, cuts, -0.22, 0.18) * drawn
    return jnp.clip(drawn, min=-reach, max=reach).astype(held_as)


def setup_inputs(seed: int = 0) -> dict:
    seeds = jax.random.split(jax.random.key(seed), 13)
    return {
        "down_in": draw_down_in(jax.random.fold_in(seeds[12], 71), 0),
        "up_in": draw_up_in(jax.random.fold_in(seeds[12], 71), 0),
        "down_cot": normal_values(seeds[2], (S, TOKENS, D), (1.0 / (M * N_DP)), 0.03125, ((0, 32), (2, 16))),
        "up_cot": normal_values(seeds[3], (S, TOKENS, D), (1.0 / (M * N_DP)), 0.03125, ((0, 32), (2, 16))),
        "adapt_a": normal_values(seeds[4], (S, D, R), D ** -0.5, 0.0625, ((0, 32), (1, 16))),
        "adapt_b": normal_values(seeds[5], (S, R, D), R ** -0.5, 1.0, ((0, 32), (2, 16))),
        "head_gain": jnp.clip(1.0 + 0.1 * jax.random.normal(seeds[6], (K, D), jnp.float32), 0.5, 1.5),
        "cand": draw_cand(jax.random.fold_in(seeds[12], 71), 0),
        "down_ids": set_ends(jax.random.randint(seeds[8], (TOKENS,), 0, CAND), jax.random.fold_in(seeds[8], 1), 0, CAND - 1).astype(jnp.int32),
        "up_ids": set_ends(jax.random.randint(seeds[9], (TOKENS,), 0, CAND), jax.random.fold_in(seeds[9], 1), 0, CAND - 1).astype(jnp.int32),
        "offsets": set_ends(jax.random.randint(seeds[10], (K,), 1, K + 1), jax.random.fold_in(seeds[10], 1), 1, K).astype(jnp.int32),
        "loss_weights": set_ends(jax.random.randint(seeds[11], (K,), 1, 5), jax.random.fold_in(seeds[11], 1), 1, 4).astype(jnp.int32),
    }


EPS = 1e-05
HIGH = lax.Precision.HIGHEST

def section_layer(inputs, proj_a, proj_b):
    scale = lax.rsqrt(lax.optimization_barrier(jnp.mean(inputs * inputs, axis=-1, keepdims=True)) + EPS)
    normed = inputs * scale
    inner = jax.nn.silu(jnp.dot(normed, proj_a, precision=HIGH))
    return inputs + jnp.dot(inner, proj_b, precision=HIGH)

def head_loss(outputs, ids, head_gain, cand, offsets, loss_weights, groups):
    rows = outputs.shape[1]
    scale = lax.rsqrt(lax.optimization_barrier(jnp.mean(outputs * outputs, axis=-1, keepdims=True)) + EPS)
    normed = outputs * scale
    cand32 = cand.astype(jnp.float32)
    classes = jnp.arange(cand.shape[0], dtype=jnp.int32)
    places = jnp.arange(rows, dtype=jnp.int32)
    weight_sum = jnp.sum(loss_weights).astype(jnp.float32)
    total = jnp.float32(0.0)
    for head in range(head_gain.shape[0]):
        logits = jnp.einsum('gmd,cd->gmc', normed * head_gain[head], cand32, precision=HIGH)
        ahead = places + offsets[head].astype(jnp.int32)
        valid = ahead < rows
        target = jnp.take(ids, jnp.clip(ahead, 0, rows - 1), axis=1)
        picked = lax.optimization_barrier(jnp.sum(jnp.where(target[..., None] == classes, logits, 0.0), axis=-1))
        entropy = jax.nn.logsumexp(logits, axis=-1) - picked
        count = (rows - offsets[head]).astype(jnp.float32)
        total = total + loss_weights[head].astype(jnp.float32) / weight_sum * jnp.sum(jnp.where(valid[None, :], entropy, 0.0)) / count
    return total / groups

def forward_one(args):
    inputs, proj_a, proj_b = args
    return section_layer(inputs.astype(jnp.float32), proj_a.astype(jnp.float32), proj_b.astype(jnp.float32)).astype(jnp.bfloat16)

def backward_one(args):
    inputs, proj_a, proj_b, cotan = args
    result, pull = jax.vjp(section_layer, inputs.astype(jnp.float32), proj_a.astype(jnp.float32), proj_b.astype(jnp.float32))
    d_in, d_a, d_b = pull(cotan)
    return (d_in.astype(jnp.bfloat16), d_a, d_b)

def reference(down_in, up_in, down_cot, up_cot, adapt_a, adapt_b, head_gain, cand, down_ids, up_ids, offsets, loss_weights):
    rev_a = adapt_a[::-1]
    rev_b = adapt_b[::-1]
    out_d = lax.map(forward_one, (down_in, adapt_a, adapt_b))
    out_u = lax.map(forward_one, (up_in, rev_a, rev_b))
    ids_d = down_ids.reshape(N_DP, M)
    ids_u = up_ids.reshape(N_DP, M)
    last_d = out_d[S - 1].astype(jnp.float32).reshape(N_DP, M, D)
    last_u = out_u[0].astype(jnp.float32).reshape(N_DP, M, D)
    loss_d, grad_d = jax.value_and_grad(head_loss)(last_d, ids_d, head_gain, cand, offsets, loss_weights, N_DP)
    loss_u, grad_u = jax.value_and_grad(head_loss)(last_u, ids_u, head_gain, cand, offsets, loss_weights, N_DP)
    cot_d = down_cot.astype(jnp.float32).at[S - 1].set(grad_d.reshape(TOKENS, D))
    cot_u = up_cot.astype(jnp.float32).at[0].set(grad_u.reshape(TOKENS, D))
    back_d, da_d, db_d = lax.map(backward_one, (down_in, adapt_a, adapt_b, cot_d))
    back_u, da_u, db_u = lax.map(backward_one, (up_in, rev_a, rev_b, cot_u))
    zeros = jnp.zeros((1, TOKENS, D), jnp.bfloat16)
    down_next = jnp.concatenate([zeros, out_d[:-1]], axis=0)
    up_next = jnp.concatenate([out_u[1:], zeros], axis=0)
    down_back = jnp.concatenate([back_d[1:], zeros], axis=0)
    up_back = jnp.concatenate([zeros, back_u[:-1]], axis=0)
    grad_a = da_d + da_u[::-1]
    grad_b = db_d + db_u[::-1]
    loss = jnp.reshape(loss_d + loss_u, (1,))
    return (down_next, up_next, down_back, up_back, grad_a, grad_b, loss)
```

```python
import jax
import jax.numpy as jnp
from jax import lax
from jax.experimental import pallas as pl
from jax.experimental.pallas import tpu as pltpu
from jax.sharding import PartitionSpec as P

EPS = 1e-05
F32 = jnp.float32
BF16 = jnp.bfloat16
HIGH = lax.Precision.HIGHEST
ROWS = 112
BACK_ROWS = 80
R = 32
LANES = 128


def nt(a, b, precision=None):
    return lax.dot_general(a, b, (((1,), (1,)), ((), ())), precision=precision, preferred_element_type=F32)


def nn(a, b, precision=None):
    return lax.dot_general(a, b, (((1,), (0,)), ((), ())), precision=precision, preferred_element_type=F32)


def tn(a, b):
    return lax.dot_general(a, b, (((0,), (0,)), ((), ())), preferred_element_type=F32)


def halves(value):
    high = value.astype(BF16)
    return high, (value - high.astype(F32)).astype(BF16)


def columns_of(gain_ref, cand_ref):
    cand = cand_ref[...].astype(F32)
    return jnp.concatenate([gain_ref[k : k + 1, :] * cand for k in range(gain_ref.shape[0])], axis=0)


def squares_row(block):
    wide = block.astype(F32)
    ones = jnp.ones((8, wide.shape[1]), BF16)
    high, low = halves(wide * wide)
    return (nt(ones, high) + nt(ones, low))[0:1, :]


def gated(weights, flag):
    return jnp.where(flag, weights.astype(F32), 0.0).astype(BF16)


def first_partial(meta, x_d, x_u, c_d, a_d, b_d, gain, cand, out):
    sections = meta[2]
    is_first = meta[1] == 0
    is_last = meta[1] == sections - 1
    chunks = out.shape[0]
    width = x_d.shape[1]
    zero = jnp.zeros((R, width), BF16)
    wx = jnp.concatenate([a_d[...], zero, gated(b_d[...], is_last), zero], axis=0)
    wc = jnp.concatenate([zero, zero, gated(b_d[...], jnp.logical_not(is_last)), zero], axis=0)
    main = nt(x_d[...], wx) + nt(c_d[...], wc)
    out[:, 0:R, :] = main.astype(BF16).reshape(chunks, R, LANES)
    rows = []
    for block in (x_d[...], x_u[...]):
        row = squares_row(block)
        high = row.astype(BF16).astype(F32)
        rows += [high, row - high]
    per = LANES // R
    pad = jnp.zeros((8, LANES), F32)
    for j in range(chunks):
        start = (j // per) * LANES
        piece = [row[:, start : start + LANES] for row in rows]
        tail = jnp.concatenate([pad] + piece + [pad[0:4]], axis=0)
        out[j, 96:ROWS, :] = tail.astype(BF16)
    out[:, 64:96, :] = jnp.zeros((chunks, R, LANES), BF16)

    def logits_of(block):
        high, low = halves(columns_of(gain, cand))
        value = nt(block, high) + nt(block, low)
        out[:, 32:64, :] = value.astype(BF16).reshape(chunks, R, LANES)

    @pl.when(is_last)
    def _():
        logits_of(x_d[...])

    @pl.when(is_first)
    def _():
        logits_of(x_u[...])

    @pl.when(jnp.logical_not(jnp.logical_or(is_first, is_last)))
    def _():
        out[:, 32:64, :] = jnp.zeros((chunks, R, LANES), BF16)


def second_partial(meta, partial, x_u, c_u, a_u, b_u, b_d, gain, cand, out):
    is_first = meta[1] == 0
    is_last = meta[1] == meta[2] - 1
    chunks = out.shape[0]
    width = x_u.shape[1]
    zero = jnp.zeros((R, width), BF16)
    wx = jnp.concatenate([zero, a_u[...], zero, gated(b_u[...], is_first)], axis=0)
    wc = jnp.concatenate([zero, zero, zero, gated(b_u[...], jnp.logical_not(is_first))], axis=0)
    main = nt(x_u[...], wx) + nt(c_u[...], wc)
    main = main.reshape(chunks, R, LANES) + partial[:, 0:R, :].astype(F32)
    out[:, 0:R, :] = main.astype(BF16)
    out[:, R:ROWS, :] = partial[:, R:ROWS, :]

    @pl.when(jnp.logical_or(is_first, is_last))
    def _():
        b_e = jnp.where(is_last, b_d[...].astype(F32), b_u[...].astype(F32)).astype(BF16)
        high, low = halves(columns_of(gain, cand))
        cross = nt(b_e, high) + nt(b_e, low)
        own = nt(b_e, b_e)
        packed = jnp.concatenate([own[8 * r : 8 * r + 8] for r in range(4)], axis=1)
        tail = jnp.concatenate([packed, jnp.zeros((8, LANES), F32)], axis=0)
        out[:, 64:96, :] = jnp.broadcast_to(cross.astype(BF16)[None], (chunks, R, LANES))
        held = partial[:, 96:ROWS, :].astype(F32) + tail[None]
        out[:, 96:ROWS, :] = held.astype(BF16)


def middle(meta, offsets, loss_weights, received, down_ids, up_ids, out):
    place = meta[0]
    is_first = meta[1] == 0
    is_last = meta[1] == meta[2] - 1
    is_end = jnp.logical_or(is_first, is_last)
    chunks = received.shape[0]
    inverse = 1.0 / meta[3].astype(F32)
    heads = LANES // R
    total = jnp.sum(received[...].astype(F32), axis=0)
    main, base_logits, cross = total[0:32], total[32:64], total[64:96]
    packed, square_rows = total[96:104], total[104:108]
    lane = lax.broadcasted_iota(jnp.int32, (R, LANES), 1)
    token = lax.broadcasted_iota(jnp.int32, (R, LANES), 0)
    base = R * lax.rem(place, LANES // R)

    def column(row):
        return jnp.sum(jnp.where(lane == base + token, row, 0.0), axis=1, keepdims=True)

    square_d = column(square_rows[0:1] + square_rows[1:2])
    square_u = column(square_rows[2:3] + square_rows[3:4])
    scale_d = lax.rsqrt(square_d * inverse + EPS)
    scale_u = lax.rsqrt(square_u * inverse + EPS)
    down_lane = lane < R
    up_lane = jnp.logical_and(lane >= R, lane < 2 * R)
    low_lane = lane < 2 * R
    scale = jnp.where(down_lane, scale_d, scale_u)
    projected = jnp.where(low_lane, main, 0.0)
    pre = projected * scale
    sigma = jax.nn.sigmoid(pre)
    act = pre * sigma

    act_e = jnp.where(is_first, act[:, R : 2 * R], act[:, 0:R])
    cot_e = jnp.where(is_first, main[:, 3 * R :], main[:, 2 * R : 3 * R])
    own = jnp.concatenate([packed[:, R * r : R * r + R] for r in range(4)], axis=0)
    act_own = nn(act_e, own, HIGH)
    out_b = cot_e + act_own
    square_e = jnp.where(is_first, square_u, square_d)
    square_e = square_e + jnp.sum(act_e * (cot_e + out_b), axis=1, keepdims=True)
    scale_e = lax.rsqrt(jnp.maximum(square_e, 0.0) * inverse + EPS)
    raw = base_logits + nn(act_e, cross, HIGH)
    logits = raw * scale_e
    block = lax.div(place, LANES // R)
    ids_d = down_ids[pl.ds(block, 1), :]
    ids_u = up_ids[pl.ds(block, 1), :]
    ids = jnp.where(is_first, ids_u, ids_d).astype(F32)
    group = lax.div(lane, R)
    within = lax.rem(lane, R)
    weight_sum = jnp.float32(0.0)
    for k in range(heads):
        weight_sum = weight_sum + loss_weights[k].astype(F32)
    top = jnp.zeros((R, LANES), F32)
    target = jnp.zeros((R, LANES), F32)
    weight = jnp.zeros((R, LANES), F32)
    for k in range(heads):
        mine = group == k
        shift = offsets[k]
        largest = jnp.max(jnp.where(mine, logits, -jnp.inf), axis=1, keepdims=True)
        wanted = jnp.sum(jnp.where(lane == base + token + shift, ids, 0.0), axis=1, keepdims=True)
        factor = loss_weights[k].astype(F32) / weight_sum / ((R - shift) * chunks).astype(F32)
        valid = jnp.where(token + shift < R, factor, 0.0)
        top = jnp.where(mine, largest, top)
        target = jnp.where(mine, wanted, target)
        weight = jnp.where(mine, valid, weight)
    power = jnp.exp(logits - top)
    below = jnp.ones((R, LANES), F32)
    for k in range(heads):
        mine = group == k
        below = jnp.where(mine, jnp.sum(jnp.where(mine, power, 0.0), axis=1, keepdims=True), below)
    hit = jnp.where(within == target.astype(jnp.int32), 1.0, 0.0)
    per_lane = hit * (top + jnp.log(below) - logits) * weight
    loss = jnp.sum(jnp.sum(per_lane, axis=1, keepdims=True), axis=0, keepdims=True)
    grad = weight * (power / below - hit)
    grad_cols = grad * scale_e
    coef_e = jnp.sum(grad * raw, axis=1, keepdims=True) * scale_e * scale_e * scale_e * inverse
    dg_e = nt(grad_cols, cross, HIGH) - coef_e * out_b

    dg = pltpu.roll(main, 2 * R, axis=1)
    dg_wide = jnp.concatenate([dg_e] * 4, axis=1)
    replace = jnp.logical_or(jnp.logical_and(is_last, down_lane), jnp.logical_and(is_first, up_lane))
    dg = jnp.where(replace, dg_wide, dg)
    d_pre = jnp.where(low_lane, dg * sigma * (1.0 + pre * (1.0 - sigma)), 0.0)
    d_scaled = d_pre * scale
    moved = d_pre * projected
    coef_d = jnp.sum(jnp.where(down_lane, moved, 0.0), axis=1, keepdims=True)
    coef_u = jnp.sum(jnp.where(up_lane, moved, 0.0), axis=1, keepdims=True)
    coef_d = coef_d * scale_d * scale_d * scale_d * inverse
    coef_u = coef_u * scale_u * scale_u * scale_u * inverse
    both = jnp.where(low_lane, act, pltpu.roll(d_scaled, 2 * R, axis=1))
    head = jnp.where(is_end, grad_cols, 0.0)

    def parts_of(row):
        high = row.astype(BF16).astype(F32)
        low = (row - high).astype(BF16).astype(F32)
        return [high, low, row - high - low]

    rows = []
    for col in (coef_d, coef_u, coef_e):
        row = jnp.sum(jnp.where(lane == token, col, 0.0), axis=0, keepdims=True)
        rows += parts_of(row)[0:2]
    rows += parts_of(jnp.broadcast_to(jnp.where(is_end, loss, 0.0), (1, LANES)))
    rows += [jnp.zeros((7, LANES), F32)]
    chunk = jnp.concatenate([both, head, jnp.concatenate(rows, axis=0)], axis=0)
    out[...] = jnp.broadcast_to(chunk.astype(BF16)[None], out.shape)


def tokens_of(received, first):
    chunks = received.shape[0]
    return received[:, first : first + R, :].reshape(chunks * R, LANES)


def coefficient(received, row):
    chunks = received.shape[0]
    lane = lax.broadcasted_iota(jnp.int32, (R, LANES), 1)
    token = lax.broadcasted_iota(jnp.int32, (R, LANES), 0)
    cols = []
    for j in range(chunks):
        rows = received[j, 64:BACK_ROWS, :].astype(F32)
        both = rows[row : row + 1] + rows[row + 1 : row + 2]
        cols.append(jnp.sum(jnp.where(lane == token, both, 0.0), axis=1, keepdims=True))
    return jnp.concatenate(cols, axis=0)


def at_rows(weights, group):
    zero = jnp.zeros_like(weights)
    return jnp.concatenate([weights if k == group else zero for k in range(LANES // R)], axis=0)


def outputs(received, x_d, x_u, b_d, b_u, y_d, y_u, loss):
    act = tokens_of(received, 0)
    y_d[...] = (x_d[...].astype(F32) + nn(act, at_rows(b_d[...], 0))).astype(BF16)
    y_u[...] = (x_u[...].astype(F32) + nn(act, at_rows(b_u[...], 1))).astype(BF16)
    rows = jnp.sum(received[:, 64:BACK_ROWS, :].astype(F32), axis=0)
    total = rows[6:7] + rows[7:8] + rows[8:9]
    loss[...] = jnp.broadcast_to(total, loss.shape)


def backward(meta, received, x_d, x_u, c_d, c_u, a_d, b_d, a_u, b_u, gain, cand, dx_d, dx_u, g_d, g_u, cot):
    is_first = meta[1] == 0
    is_last = meta[1] == meta[2] - 1
    act = tokens_of(received, 0)
    work = (
        (1, x_u, c_u, a_u, b_u, dx_u, g_u, is_first),
        (0, x_d, c_d, a_d, b_d, dx_d, g_d, is_last),
    )
    for side, x, c, a, b, dx, g, end in work:
        cot[...] = c[...].astype(F32)

        @pl.when(end)
        def _():
            high, low = halves(columns_of(gain, cand))
            grad = tokens_of(received, 32)
            final = x[...].astype(F32) + nn(act, at_rows(b[...], side))
            cot[...] = nn(grad, high) + nn(grad, low) - coefficient(received, 4) * final

        held = cot[...]
        wide = x[...].astype(F32)
        back = held + nn(act, at_rows(a[...], 2 + side)) - coefficient(received, 2 * side) * wide
        dx[...] = back.astype(BF16)
        by_cot = tn(act, held.astype(BF16))
        by_x = tn(act, x[...])
        grads = jnp.concatenate(
            [by_x[64 + R * side : 64 + R * side + R], by_cot[R * side : R * side + R]], axis=0
        )
        g[...] = grads.astype(g.dtype)


def finish(g_d, mate, losses, grad_a, grad_b, loss):
    total = g_d[...] + mate[...].astype(F32)
    grad_a[...] = total[0:R]
    grad_b[...] = total[R : 2 * R]
    loss[0] = jnp.sum(losses[:, 0:1])


def shards(
    down_in,
    up_in,
    down_cot,
    up_cot,
    adapt_a,
    adapt_b,
    head_gain,
    cand,
    down_ids,
    up_ids,
    offsets,
    loss_weights,
):
    sections = lax.axis_size("section")
    groups = lax.axis_size("dp")
    position = lax.axis_index("section")
    place = lax.axis_index("dp")
    x_d, x_u, c_d, c_u = down_in[0], up_in[0], down_cot[0], up_cot[0]
    tokens, local_width = x_d.shape
    a_d = adapt_a[0].T
    b_d = adapt_b[0]
    mirror = [(i, sections - 1 - i) for i in range(sections)]
    a_u = lax.ppermute(a_d, "section", mirror)
    b_u = lax.ppermute(b_d, "section", mirror)
    whole = jnp.int32(sections), jnp.int32(head_gain.shape[1])
    meta = jnp.stack([place.astype(jnp.int32), position.astype(jnp.int32), *whole])
    gain_part = lax.dynamic_slice_in_dim(head_gain, place * local_width, local_width, 1)
    cand_part = lax.dynamic_slice_in_dim(cand, place * local_width, local_width, 1)
    smem = pl.BlockSpec(memory_space=pltpu.SMEM)
    vmem = pl.BlockSpec(memory_space=pltpu.VMEM)
    params = pltpu.CompilerParams(vmem_limit_bytes=48 << 20)

    send = jax.ShapeDtypeStruct((groups, ROWS, LANES), BF16)
    partial = pl.pallas_call(
        first_partial,
        out_shape=send,
        in_specs=[smem] + [vmem] * 7,
        out_specs=vmem,
        compiler_params=params,
    )(meta, x_d, x_u, c_d, a_d, b_d, gain_part, cand_part)
    partial = pl.pallas_call(
        second_partial,
        out_shape=send,
        in_specs=[smem] + [vmem] * 8,
        out_specs=vmem,
        compiler_params=params,
    )(meta, partial, x_u, c_u, a_u, b_u, b_d, gain_part, cand_part)
    received = lax.all_to_all(partial, "dp", 0, 0)

    back = pl.pallas_call(
        middle,
        out_shape=jax.ShapeDtypeStruct((groups, BACK_ROWS, LANES), BF16),
        in_specs=[smem] * 3 + [vmem] * 3,
        out_specs=vmem,
        compiler_params=params,
    )(
        meta,
        offsets,
        loss_weights,
        received,
        down_ids.reshape(tokens // LANES, LANES),
        up_ids.reshape(tokens // LANES, LANES),
    )
    gathered = lax.all_to_all(back, "dp", 0, 0)

    wide = jax.ShapeDtypeStruct((tokens, local_width), BF16)
    y_d, y_u, loss_rows = pl.pallas_call(
        outputs,
        out_shape=(wide, wide, jax.ShapeDtypeStruct((sections, LANES), F32)),
        in_specs=[vmem] * 5,
        out_specs=(vmem,) * 3,
        compiler_params=params,
    )(gathered, x_d, x_u, b_d, b_u)
    ahead = [(i, i + 1) for i in range(sections - 1)]
    behind = [(i + 1, i) for i in range(sections - 1)]
    down_next = lax.ppermute(y_d, "section", ahead)
    up_next = lax.ppermute(y_u, "section", behind)

    dx_d, dx_u, g_d, g_u = pl.pallas_call(
        backward,
        out_shape=(
            wide,
            wide,
            jax.ShapeDtypeStruct((2 * R, local_width), F32),
            jax.ShapeDtypeStruct((2 * R, local_width), BF16),
        ),
        in_specs=[smem] + [vmem] * 11,
        out_specs=(vmem,) * 4,
        scratch_shapes=[pltpu.VMEM((tokens, local_width), F32)],
        compiler_params=params,
    )(meta, gathered, x_d, x_u, c_d, c_u, a_d, b_d, a_u, b_u, gain_part, cand_part)
    mate = lax.ppermute(g_u, "section", mirror)
    down_back = lax.ppermute(dx_d, "section", behind)
    up_back = lax.ppermute(dx_u, "section", ahead)
    losses = lax.all_to_all(loss_rows, "section", 0, 0, tiled=True)
    grad_a, grad_b, loss = pl.pallas_call(
        finish,
        out_shape=(
            jax.ShapeDtypeStruct((R, local_width), F32),
            jax.ShapeDtypeStruct((R, local_width), F32),
            jax.ShapeDtypeStruct((1,), F32),
        ),
        in_specs=[vmem] * 3,
        out_specs=(vmem, vmem, smem),
        compiler_params=params,
    )(g_d, mate, losses)
    return (
        down_next[None],
        up_next[None],
        down_back[None],
        up_back[None],
        grad_a.T[None],
        grad_b[None],
        loss,
    )


def solution(mesh):
    in_specs = (
        P("section", None, "dp"),
        P("section", None, "dp"),
        P("section", None, "dp"),
        P("section", None, "dp"),
        P("section", "dp", None),
        P("section", None, "dp"),
        P(),
        P(),
        P(),
        P(),
        P(),
        P(),
    )
    out_specs = (
        P("section", None, "dp"),
        P("section", None, "dp"),
        P("section", None, "dp"),
        P("section", None, "dp"),
        P("section", "dp", None),
        P("section", None, "dp"),
        P(),
    )
    return jax.shard_map(shards, mesh=mesh, in_specs=in_specs, out_specs=out_specs, check_vma=False)
```

```python
import jax
import jax.numpy as jnp
from jax import lax
from jax.experimental import pallas as pl
from jax.experimental.pallas import tpu as pltpu
from jax.sharding import PartitionSpec as P

EPS = 1e-05
F32 = jnp.float32
BF16 = jnp.bfloat16
HIGH = lax.Precision.HIGHEST
ROWS = 112
BACK_ROWS = 80
R = 32
LANES = 128


def nt(a, b, precision=None):
    return lax.dot_general(a, b, (((1,), (1,)), ((), ())), precision=precision, preferred_element_type=F32)


def nn(a, b, precision=None):
    return lax.dot_general(a, b, (((1,), (0,)), ((), ())), precision=precision, preferred_element_type=F32)


def tn(a, b):
    return lax.dot_general(a, b, (((0,), (0,)), ((), ())), preferred_element_type=F32)


def halves(value):
    high = value.astype(BF16)
    return high, (value - high.astype(F32)).astype(BF16)


def columns_of(gain_ref, cand_ref):
    cand = cand_ref[...].astype(F32)
    return jnp.concatenate([gain_ref[k : k + 1, :] * cand for k in range(gain_ref.shape[0])], axis=0)


def squares_row(block):
    wide = block.astype(F32)
    ones = jnp.ones((8, wide.shape[1]), BF16)
    high, low = halves(wide * wide)
    return (nt(ones, high) + nt(ones, low))[0:1, :]


def gated(weights, flag):
    return jnp.where(flag, weights.astype(F32), 0.0).astype(BF16)


def in_hbm(value):
    return pltpu.with_memory_space_constraint(value, pltpu.HBM)


def packed(a_hbm, b_hbm, w, sems):
    copies = [
        pltpu.make_async_copy(a_hbm, w.at[0:R], sems.at[0]),
        pltpu.make_async_copy(b_hbm, w.at[R : 2 * R], sems.at[1]),
    ]
    for copy in copies:
        copy.start()
    for copy in copies:
        copy.wait()


def first_partial(
    meta,
    x_d_hbm,
    x_u_hbm,
    c_d_hbm,
    c_u_hbm,
    gain_hbm,
    cand_hbm,
    ids_d_hbm,
    ids_u_hbm,
    w_d,
    out,
    x_d,
    x_u,
    c_d,
    c_u,
    gain,
    cand,
    ids_d,
    ids_u,
    sems,
):
    sections = meta[2]
    is_first = meta[1] == 0
    is_last = meta[1] == sections - 1
    chunks = out.shape[0]
    width = x_d.shape[1]
    here = pl.ds(pl.multiple_of(meta[0] * width, width), width)
    get_x_d = pltpu.make_async_copy(x_d_hbm, x_d, sems.at[0])
    get_c_d = pltpu.make_async_copy(c_d_hbm, c_d, sems.at[1])
    get_x_u = pltpu.make_async_copy(x_u_hbm, x_u, sems.at[2])
    get_c_u = pltpu.make_async_copy(c_u_hbm, c_u, sems.at[3])
    get_gain = pltpu.make_async_copy(gain_hbm.at[:, here], gain, sems.at[4])
    get_cand = pltpu.make_async_copy(cand_hbm.at[:, here], cand, sems.at[5])
    get_ids_d = pltpu.make_async_copy(ids_d_hbm, ids_d, sems.at[6])
    get_ids_u = pltpu.make_async_copy(ids_u_hbm, ids_u, sems.at[7])
    for copy in (get_x_d, get_c_d, get_x_u, get_gain, get_cand, get_c_u, get_ids_d, get_ids_u):
        copy.start()
    a_d, b_d = w_d[0:R], w_d[R : 2 * R]
    zero = jnp.zeros((R, width), BF16)
    wx = jnp.concatenate([a_d, zero, gated(b_d, is_last), zero], axis=0)
    wc = jnp.concatenate([zero, zero, gated(b_d, jnp.logical_not(is_last)), zero], axis=0)
    out[:, 64:96, :] = jnp.zeros((chunks, R, LANES), BF16)
    get_x_d.wait()
    get_c_d.wait()
    main = nt(x_d[...], wx) + nt(c_d[...], wc)
    out[:, 0:R, :] = main.astype(BF16).reshape(chunks, R, LANES)
    get_x_u.wait()
    rows = []
    for block in (x_d[...], x_u[...]):
        row = squares_row(block)
        high = row.astype(BF16).astype(F32)
        rows += [high, row - high]
    per = LANES // R
    pad = jnp.zeros((8, LANES), F32)
    for j in range(chunks):
        start = (j // per) * LANES
        piece = [row[:, start : start + LANES] for row in rows]
        tail = jnp.concatenate([pad] + piece + [pad[0:4]], axis=0)
        out[j, 96:ROWS, :] = tail.astype(BF16)
    get_gain.wait()
    get_cand.wait()

    def logits_of(block):
        high, low = halves(columns_of(gain, cand))
        value = nt(block, high) + nt(block, low)
        out[:, 32:64, :] = value.astype(BF16).reshape(chunks, R, LANES)

    @pl.when(is_last)
    def _():
        logits_of(x_d[...])

    @pl.when(is_first)
    def _():
        logits_of(x_u[...])

    @pl.when(jnp.logical_not(jnp.logical_or(is_first, is_last)))
    def _():
        out[:, 32:64, :] = jnp.zeros((chunks, R, LANES), BF16)

    get_c_u.wait()
    get_ids_d.wait()
    get_ids_u.wait()


def second_partial(meta, partial, x_u, c_u, w_u, w_d, gain, cand, out):
    is_first = meta[1] == 0
    is_last = meta[1] == meta[2] - 1
    chunks = out.shape[0]
    width = x_u.shape[1]
    a_u, b_u = w_u[0:R], w_u[R : 2 * R]
    zero = jnp.zeros((R, width), BF16)
    wx = jnp.concatenate([zero, a_u, zero, gated(b_u, is_first)], axis=0)
    wc = jnp.concatenate([zero, zero, zero, gated(b_u, jnp.logical_not(is_first))], axis=0)
    main = nt(x_u[...], wx) + nt(c_u[...], wc)
    main = main.reshape(chunks, R, LANES) + partial[:, 0:R, :].astype(F32)
    out[:, 0:R, :] = main.astype(BF16)
    out[:, R:ROWS, :] = partial[:, R:ROWS, :]

    @pl.when(jnp.logical_or(is_first, is_last))
    def _():
        b_d = w_d[R : 2 * R]
        b_e = jnp.where(is_last, b_d.astype(F32), b_u.astype(F32)).astype(BF16)
        high, low = halves(columns_of(gain, cand))
        cross = nt(b_e, high) + nt(b_e, low)
        own = nt(b_e, b_e)
        folded = jnp.concatenate([own[8 * r : 8 * r + 8] for r in range(4)], axis=1)
        tail = jnp.concatenate([folded, jnp.zeros((8, LANES), F32)], axis=0)
        out[:, 64:96, :] = jnp.broadcast_to(cross.astype(BF16)[None], (chunks, R, LANES))
        held = partial[:, 96:ROWS, :].astype(F32) + tail[None]
        out[:, 96:ROWS, :] = held.astype(BF16)


def middle(meta, received, down_ids, up_ids, out):
    place = meta[0]
    is_first = meta[1] == 0
    is_last = meta[1] == meta[2] - 1
    is_end = jnp.logical_or(is_first, is_last)
    chunks = received.shape[0]
    inverse = 1.0 / meta[3].astype(F32)
    heads = LANES // R
    offsets = [meta[4 + k] for k in range(heads)]
    loss_weights = [meta[4 + heads + k] for k in range(heads)]
    total = jnp.sum(received[...].astype(F32), axis=0)
    main, base_logits, cross = total[0:32], total[32:64], total[64:96]
    folded, square_rows = total[96:104], total[104:108]
    lane = lax.broadcasted_iota(jnp.int32, (R, LANES), 1)
    token = lax.broadcasted_iota(jnp.int32, (R, LANES), 0)
    base = R * lax.rem(place, LANES // R)

    def column(row):
        return jnp.sum(jnp.where(lane == base + token, row, 0.0), axis=1, keepdims=True)

    square_d = column(square_rows[0:1] + square_rows[1:2])
    square_u = column(square_rows[2:3] + square_rows[3:4])
    scale_d = lax.rsqrt(square_d * inverse + EPS)
    scale_u = lax.rsqrt(square_u * inverse + EPS)
    down_lane = lane < R
    up_lane = jnp.logical_and(lane >= R, lane < 2 * R)
    low_lane = lane < 2 * R
    scale = jnp.where(down_lane, scale_d, scale_u)
    projected = jnp.where(low_lane, main, 0.0)
    pre = projected * scale
    sigma = jax.nn.sigmoid(pre)
    act = pre * sigma

    act_e = jnp.where(is_first, act[:, R : 2 * R], act[:, 0:R])
    cot_e = jnp.where(is_first, main[:, 3 * R :], main[:, 2 * R : 3 * R])
    own = jnp.concatenate([folded[:, R * r : R * r + R] for r in range(4)], axis=0)
    act_own = nn(act_e, own, HIGH)
    out_b = cot_e + act_own
    square_e = jnp.where(is_first, square_u, square_d)
    square_e = square_e + jnp.sum(act_e * (cot_e + out_b), axis=1, keepdims=True)
    scale_e = lax.rsqrt(jnp.maximum(square_e, 0.0) * inverse + EPS)
    raw = base_logits + nn(act_e, cross, HIGH)
    logits = raw * scale_e
    block = lax.div(place, LANES // R)
    ids_d = down_ids[pl.ds(block, 1), :]
    ids_u = up_ids[pl.ds(block, 1), :]
    ids = jnp.where(is_first, ids_u, ids_d).astype(F32)
    group = lax.div(lane, R)
    within = lax.rem(lane, R)
    weight_sum = jnp.float32(0.0)
    for k in range(heads):
        weight_sum = weight_sum + loss_weights[k].astype(F32)
    top = jnp.zeros((R, LANES), F32)
    target = jnp.zeros((R, LANES), F32)
    weight = jnp.zeros((R, LANES), F32)
    for k in range(heads):
        mine = group == k
        shift = offsets[k]
        largest = jnp.max(jnp.where(mine, logits, -jnp.inf), axis=1, keepdims=True)
        wanted = jnp.sum(jnp.where(lane == base + token + shift, ids, 0.0), axis=1, keepdims=True)
        factor = loss_weights[k].astype(F32) / weight_sum / ((R - shift) * chunks).astype(F32)
        valid = jnp.where(token + shift < R, factor, 0.0)
        top = jnp.where(mine, largest, top)
        target = jnp.where(mine, wanted, target)
        weight = jnp.where(mine, valid, weight)
    power = jnp.exp(logits - top)
    below = jnp.ones((R, LANES), F32)
    for k in range(heads):
        mine = group == k
        below = jnp.where(mine, jnp.sum(jnp.where(mine, power, 0.0), axis=1, keepdims=True), below)
    hit = jnp.where(within == target.astype(jnp.int32), 1.0, 0.0)
    per_lane = hit * (top + jnp.log(below) - logits) * weight
    loss = jnp.sum(jnp.sum(per_lane, axis=1, keepdims=True), axis=0, keepdims=True)
    grad = weight * (power / below - hit)
    grad_cols = grad * scale_e
    coef_e = jnp.sum(grad * raw, axis=1, keepdims=True) * scale_e * scale_e * scale_e * inverse
    dg_e = nt(grad_cols, cross, HIGH) - coef_e * out_b

    dg = pltpu.roll(main, 2 * R, axis=1)
    dg_wide = jnp.concatenate([dg_e] * 4, axis=1)
    replace = jnp.logical_or(jnp.logical_and(is_last, down_lane), jnp.logical_and(is_first, up_lane))
    dg = jnp.where(replace, dg_wide, dg)
    d_pre = jnp.where(low_lane, dg * sigma * (1.0 + pre * (1.0 - sigma)), 0.0)
    d_scaled = d_pre * scale
    moved = d_pre * projected
    coef_d = jnp.sum(jnp.where(down_lane, moved, 0.0), axis=1, keepdims=True)
    coef_u = jnp.sum(jnp.where(up_lane, moved, 0.0), axis=1, keepdims=True)
    coef_d = coef_d * scale_d * scale_d * scale_d * inverse
    coef_u = coef_u * scale_u * scale_u * scale_u * inverse
    both = jnp.where(low_lane, act, pltpu.roll(d_scaled, 2 * R, axis=1))
    head = jnp.where(is_end, grad_cols, 0.0)

    def parts_of(row):
        high = row.astype(BF16).astype(F32)
        low = (row - high).astype(BF16).astype(F32)
        return [high, low, row - high - low]

    rows = []
    for col in (coef_d, coef_u, coef_e):
        row = jnp.sum(jnp.where(lane == token, col, 0.0), axis=0, keepdims=True)
        rows += parts_of(row)[0:2]
    rows += parts_of(jnp.broadcast_to(jnp.where(is_end, loss, 0.0), (1, LANES)))
    rows += [jnp.zeros((7, LANES), F32)]
    chunk = jnp.concatenate([both, head, jnp.concatenate(rows, axis=0)], axis=0)
    out[...] = jnp.broadcast_to(chunk.astype(BF16)[None], out.shape)


def tokens_of(received, first):
    chunks = received.shape[0]
    return received[:, first : first + R, :].reshape(chunks * R, LANES)


def coefficient(received, row):
    chunks = received.shape[0]
    lane = lax.broadcasted_iota(jnp.int32, (R, LANES), 1)
    token = lax.broadcasted_iota(jnp.int32, (R, LANES), 0)
    cols = []
    for j in range(chunks):
        rows = received[j, 64:BACK_ROWS, :].astype(F32)
        both = rows[row : row + 1] + rows[row + 1 : row + 2]
        cols.append(jnp.sum(jnp.where(lane == token, both, 0.0), axis=1, keepdims=True))
    return jnp.concatenate(cols, axis=0)


def at_rows(weights, group):
    zero = jnp.zeros_like(weights)
    return jnp.concatenate([weights if k == group else zero for k in range(LANES // R)], axis=0)


def backward(meta, received, x_d, x_u, c_d, c_u, w_d, w_u, gain, cand, ahead, behind, g_d, g_u, loss, cot):
    is_first = meta[1] == 0
    is_last = meta[1] == meta[2] - 1
    act = tokens_of(received, 0)
    work = (
        (1, x_u, c_u, w_u, behind.at[0], ahead.at[1], g_u, is_first),
        (0, x_d, c_d, w_d, ahead.at[0], behind.at[1], g_d, is_last),
    )
    for side, x, c, w, y, dx, g, end in work:
        final = x[...].astype(F32) + nn(act, at_rows(w[R : 2 * R], side))
        y[...] = final.astype(BF16)
        cot[...] = c[...].astype(F32)

        @pl.when(end)
        def _():
            high, low = halves(columns_of(gain, cand))
            grad = tokens_of(received, 32)
            again = x[...].astype(F32) + nn(act, at_rows(w[R : 2 * R], side))
            cot[...] = nn(grad, high) + nn(grad, low) - coefficient(received, 4) * again

        held = cot[...]
        wide = x[...].astype(F32)
        back = held + nn(act, at_rows(w[0:R], 2 + side)) - coefficient(received, 2 * side) * wide
        dx[...] = back.astype(BF16)
        by_cot = tn(act, held.astype(BF16))
        by_x = tn(act, x[...])
        grads = jnp.concatenate(
            [by_x[64 + R * side : 64 + R * side + R], by_cot[R * side : R * side + R]], axis=0
        )
        g[...] = grads.astype(g.dtype)
    rows = jnp.sum(received[:, 64:BACK_ROWS, :].astype(F32), axis=0)
    total = rows[6:7] + rows[7:8] + rows[8:9]
    loss[...] = jnp.broadcast_to(total, loss.shape)


def finish(ahead, behind, g_d, mate, losses, down_next, up_next, down_back, up_back, grad_a, grad_b, loss, sems):
    copies = [
        pltpu.make_async_copy(ahead.at[0], down_next, sems.at[0]),
        pltpu.make_async_copy(behind.at[0], up_next, sems.at[1]),
        pltpu.make_async_copy(behind.at[1], down_back, sems.at[2]),
        pltpu.make_async_copy(ahead.at[1], up_back, sems.at[3]),
    ]
    for copy in copies:
        copy.start()
    total = g_d[...] + mate[...].astype(F32)
    grad_a[...] = total[0:R]
    grad_b[...] = total[R : 2 * R]
    loss[0] = jnp.sum(losses[:, 0:1])
    for copy in copies:
        copy.wait()


def shards(
    down_in,
    up_in,
    down_cot,
    up_cot,
    adapt_a,
    adapt_b,
    head_gain,
    cand,
    down_ids,
    up_ids,
    offsets,
    loss_weights,
):
    sections = lax.axis_size("section")
    groups = lax.axis_size("dp")
    position = lax.axis_index("section")
    place = lax.axis_index("dp")
    tokens, local_width = down_in.shape[1:]
    heads, candidates = head_gain.shape[0], cand.shape[0]
    mirror = [(i, sections - 1 - i) for i in range(sections)]
    further = [(i, i + 1) for i in range(sections - 1)]
    nearer = [(i + 1, i) for i in range(sections - 1)]
    smem = pl.BlockSpec(memory_space=pltpu.SMEM)
    vmem = pl.BlockSpec(memory_space=pltpu.VMEM)
    hbm = pl.BlockSpec(memory_space=pltpu.HBM)
    params = pltpu.CompilerParams(vmem_limit_bytes=48 << 20)
    shape = jax.ShapeDtypeStruct
    wide = shape((tokens, local_width), BF16)
    both = shape((2, tokens, local_width), BF16)

    w_d = pl.pallas_call(
        packed,
        out_shape=shape((2 * R, local_width), BF16),
        in_specs=[hbm] * 2,
        out_specs=vmem,
        scratch_shapes=[pltpu.SemaphoreType.DMA((2,))],
        compiler_params=params,
    )(in_hbm(adapt_a[0].T), in_hbm(adapt_b[0]))
    w_u = lax.ppermute(w_d, "section", mirror)
    sizes = jnp.int32(sections), jnp.int32(head_gain.shape[1])
    meta = jnp.stack([place.astype(jnp.int32), position.astype(jnp.int32), *sizes])
    meta = jnp.concatenate([meta, offsets, loss_weights])
    id_rows = (tokens // LANES, LANES)
    ids = down_ids.reshape(id_rows), up_ids.reshape(id_rows)
    fetched = (down_in[0], up_in[0], down_cot[0], up_cot[0], head_gain, cand, *ids)

    send = shape((groups, ROWS, LANES), BF16)
    partial, x_d, x_u, c_d, c_u, gain_part, cand_part, ids_d, ids_u = pl.pallas_call(
        first_partial,
        out_shape=(
            send,
            wide,
            wide,
            wide,
            wide,
            shape((heads, local_width), F32),
            shape((candidates, local_width), BF16),
            shape(id_rows, jnp.int32),
            shape(id_rows, jnp.int32),
        ),
        in_specs=[smem] + [hbm] * 8 + [vmem],
        out_specs=(vmem,) * 9,
        scratch_shapes=[pltpu.SemaphoreType.DMA((8,))],
        compiler_params=params,
    )(meta, *(in_hbm(held) for held in fetched), w_d)
    partial = pl.pallas_call(
        second_partial,
        out_shape=send,
        in_specs=[smem] + [vmem] * 7,
        out_specs=vmem,
        compiler_params=params,
    )(meta, partial, x_u, c_u, w_u, w_d, gain_part, cand_part)
    received = lax.all_to_all(partial, "dp", 0, 0)

    back = pl.pallas_call(
        middle,
        out_shape=shape((groups, BACK_ROWS, LANES), BF16),
        in_specs=[smem] + [vmem] * 3,
        out_specs=vmem,
        compiler_params=params,
    )(meta, received, ids_d, ids_u)
    gathered = lax.all_to_all(back, "dp", 0, 0)

    ahead, behind, g_d, g_u, loss_rows = pl.pallas_call(
        backward,
        out_shape=(
            both,
            both,
            shape((2 * R, local_width), F32),
            shape((2 * R, local_width), BF16),
            shape((sections, LANES), F32),
        ),
        in_specs=[smem] + [vmem] * 9,
        out_specs=(vmem,) * 5,
        scratch_shapes=[pltpu.VMEM((tokens, local_width), F32)],
        compiler_params=params,
    )(meta, gathered, x_d, x_u, c_d, c_u, w_d, w_u, gain_part, cand_part)
    ahead = lax.ppermute(ahead, "section", further)
    behind = lax.ppermute(behind, "section", nearer)
    mate = lax.ppermute(g_u, "section", mirror)
    losses = lax.all_to_all(loss_rows, "section", 0, 0, tiled=True)
    down_next, up_next, down_back, up_back, grad_a, grad_b, loss = pl.pallas_call(
        finish,
        out_shape=(
            wide,
            wide,
            wide,
            wide,
            shape((R, local_width), F32),
            shape((R, local_width), F32),
            shape((1,), F32),
        ),
        in_specs=[vmem] * 5,
        out_specs=(hbm,) * 4 + (vmem, vmem, smem),
        scratch_shapes=[pltpu.SemaphoreType.DMA((4,))],
        compiler_params=params,
    )(ahead, behind, g_d, mate, losses)
    return (
        down_next[None],
        up_next[None],
        down_back[None],
        up_back[None],
        grad_a.T[None],
        grad_b[None],
        loss,
    )


def solution(mesh):
    in_specs = (
        P("section", None, "dp"),
        P("section", None, "dp"),
        P("section", None, "dp"),
        P("section", None, "dp"),
        P("section", "dp", None),
        P("section", None, "dp"),
        P(),
        P(),
        P(),
        P(),
        P(),
        P(),
    )
    out_specs = (
        P("section", None, "dp"),
        P("section", None, "dp"),
        P("section", None, "dp"),
        P("section", None, "dp"),
        P("section", "dp", None),
        P("section", None, "dp"),
        P(),
    )
    return jax.shard_map(shards, mesh=mesh, in_specs=in_specs, out_specs=out_specs, check_vma=False)
```

```python
import jax
import jax.numpy as jnp
from jax import lax
from jax.experimental import pallas as pl
from jax.experimental.pallas import tpu as pltpu
from jax.sharding import PartitionSpec as P

EPS = 1e-05
F32 = jnp.float32
BF16 = jnp.bfloat16
HIGH = lax.Precision.HIGHEST
R = 32
M = 32
LANES = 128
PER = 64
CROSS = 2 * PER
EXTRA = CROSS + R
ROWS = EXTRA + 16
BACK_ROWS = 2 * PER + 16


def nt(a, b, precision=None):
    return lax.dot_general(a, b, (((1,), (1,)), ((), ())), precision=precision, preferred_element_type=F32)


def nn(a, b, precision=None):
    return lax.dot_general(a, b, (((1,), (0,)), ((), ())), precision=precision, preferred_element_type=F32)


def tn(a, b):
    return lax.dot_general(a, b, (((0,), (0,)), ((), ())), preferred_element_type=F32)


def halves(value):
    high = value.astype(BF16)
    return high, (value - high.astype(F32)).astype(BF16)


def columns_of(gain_ref, cand_ref):
    cand = cand_ref[...].astype(F32)
    return jnp.concatenate([gain_ref[k : k + 1, :] * cand for k in range(gain_ref.shape[0])], axis=0)


def squares_row(block):
    wide = block.astype(F32)
    ones = jnp.ones((8, wide.shape[1]), BF16)
    high, low = halves(wide * wide)
    return (nt(ones, high) + nt(ones, low))[0:1, :]


def gated(weights, flag):
    return jnp.where(flag, weights.astype(F32), 0.0).astype(BF16)


def in_hbm(value):
    return pltpu.with_memory_space_constraint(value, pltpu.HBM)


def packed(a_hbm, b_hbm, w, sems):
    copies = [
        pltpu.make_async_copy(a_hbm, w.at[0:R], sems.at[0]),
        pltpu.make_async_copy(b_hbm, w.at[R : 2 * R], sems.at[1]),
    ]
    for copy in copies:
        copy.start()
    for copy in copies:
        copy.wait()


def first_partial(
    meta,
    x_d_hbm,
    x_u_hbm,
    c_d_hbm,
    c_u_hbm,
    gain_hbm,
    cand_hbm,
    ids_d_hbm,
    ids_u_hbm,
    w_d,
    out,
    x_d,
    x_u,
    c_d,
    c_u,
    gain,
    cand,
    ids_d,
    ids_u,
    sems,
):
    sections = meta[2]
    is_first = meta[1] == 0
    is_last = meta[1] == sections - 1
    chunks = out.shape[0]
    width = x_d.shape[1]
    here = pl.ds(pl.multiple_of(meta[0] * width, width), width)
    get_x_d = pltpu.make_async_copy(x_d_hbm, x_d, sems.at[0])
    get_c_d = pltpu.make_async_copy(c_d_hbm, c_d, sems.at[1])
    get_x_u = pltpu.make_async_copy(x_u_hbm, x_u, sems.at[2])
    get_c_u = pltpu.make_async_copy(c_u_hbm, c_u, sems.at[3])
    get_gain = pltpu.make_async_copy(gain_hbm.at[:, here], gain, sems.at[4])
    get_cand = pltpu.make_async_copy(cand_hbm.at[:, here], cand, sems.at[5])
    get_ids_d = pltpu.make_async_copy(ids_d_hbm, ids_d, sems.at[6])
    get_ids_u = pltpu.make_async_copy(ids_u_hbm, ids_u, sems.at[7])
    for copy in (get_x_d, get_c_d, get_x_u, get_gain, get_cand, get_c_u, get_ids_d, get_ids_u):
        copy.start()
    a_d, b_d = w_d[0:R], w_d[R : 2 * R]
    zero = jnp.zeros((R, width), BF16)
    wx = jnp.concatenate([a_d, zero, gated(b_d, is_last), zero], axis=0)
    wc = jnp.concatenate([zero, zero, gated(b_d, jnp.logical_not(is_last)), zero], axis=0)
    out[:, CROSS:EXTRA, :] = jnp.zeros((chunks, R, LANES), BF16)
    get_x_d.wait()
    get_c_d.wait()
    main = nt(x_d[...], wx) + nt(c_d[...], wc)
    out[:, 0:PER, :] = main.astype(BF16).reshape(chunks, PER, LANES)
    get_x_u.wait()
    rows = []
    for block in (x_d[...], x_u[...]):
        row = squares_row(block)
        high = row.astype(BF16).astype(F32)
        rows += [high, row - high]
    per = LANES // PER
    pad = jnp.zeros((8, LANES), F32)
    for j in range(chunks):
        start = (j // per) * LANES
        piece = [row[:, start : start + LANES] for row in rows]
        tail = jnp.concatenate([pad] + piece + [pad[0:4]], axis=0)
        out[j, EXTRA:ROWS, :] = tail.astype(BF16)
    get_gain.wait()
    get_cand.wait()

    def logits_of(block):
        high, low = halves(columns_of(gain, cand))
        value = nt(block, high) + nt(block, low)
        out[:, PER:CROSS, :] = value.astype(BF16).reshape(chunks, PER, LANES)

    @pl.when(is_last)
    def _():
        logits_of(x_d[...])

    @pl.when(is_first)
    def _():
        logits_of(x_u[...])

    @pl.when(jnp.logical_not(jnp.logical_or(is_first, is_last)))
    def _():
        out[:, PER:CROSS, :] = jnp.zeros((chunks, PER, LANES), BF16)

    get_c_u.wait()
    get_ids_d.wait()
    get_ids_u.wait()


def second_partial(meta, partial, x_u, c_u, w_u, w_d, gain, cand, out):
    is_first = meta[1] == 0
    is_last = meta[1] == meta[2] - 1
    chunks = out.shape[0]
    width = x_u.shape[1]
    a_u, b_u = w_u[0:R], w_u[R : 2 * R]
    zero = jnp.zeros((R, width), BF16)
    wx = jnp.concatenate([zero, a_u, zero, gated(b_u, is_first)], axis=0)
    wc = jnp.concatenate([zero, zero, zero, gated(b_u, jnp.logical_not(is_first))], axis=0)
    main = nt(x_u[...], wx) + nt(c_u[...], wc)
    main = main.reshape(chunks, PER, LANES) + partial[:, 0:PER, :].astype(F32)
    out[:, 0:PER, :] = main.astype(BF16)
    out[:, PER:ROWS, :] = partial[:, PER:ROWS, :]

    @pl.when(jnp.logical_or(is_first, is_last))
    def _():
        b_d = w_d[R : 2 * R]
        b_e = jnp.where(is_last, b_d.astype(F32), b_u.astype(F32)).astype(BF16)
        high, low = halves(columns_of(gain, cand))
        cross = nt(b_e, high) + nt(b_e, low)
        own = nt(b_e, b_e)
        folded = jnp.concatenate([own[8 * r : 8 * r + 8] for r in range(4)], axis=1)
        tail = jnp.concatenate([folded, jnp.zeros((8, LANES), F32)], axis=0)
        out[:, CROSS:EXTRA, :] = jnp.broadcast_to(cross.astype(BF16)[None], (chunks, R, LANES))
        held = partial[:, EXTRA:ROWS, :].astype(F32) + tail[None]
        out[:, EXTRA:ROWS, :] = held.astype(BF16)


def gathered_sum(received, out):
    total = jnp.sum(received[...].astype(F32), axis=0)
    folded = total[EXTRA : EXTRA + 8]
    rows = [folded]
    for side in range(2):
        first = EXTRA + 8 + 2 * side
        row = total[first : first + 1] + total[first + 1 : first + 2]
        high = row.astype(BF16).astype(F32)
        rows += [high, row - high]
    rows += [jnp.zeros((4, LANES), F32)]
    out[0:EXTRA] = total[0:EXTRA].astype(BF16)
    out[EXTRA:ROWS] = jnp.concatenate(rows, axis=0).astype(BF16)


def middle(meta, received, down_ids, up_ids, out):
    chunks = out.shape[0]
    place = lax.rem(meta[0], chunks)
    is_first = meta[1] == 0
    is_last = meta[1] == meta[2] - 1
    is_end = jnp.logical_or(is_first, is_last)
    inverse = 1.0 / meta[3].astype(F32)
    heads = LANES // R
    offsets = [meta[4 + k] for k in range(heads)]
    loss_weights = [meta[4 + heads + k] for k in range(heads)]
    total = received[0].astype(F32) + received[1].astype(F32)
    main, base_logits, cross = total[0:PER], total[PER:CROSS], total[CROSS:EXTRA]
    folded, square_rows = total[EXTRA : EXTRA + 8], total[EXTRA + 8 : EXTRA + 12]
    lane = lax.broadcasted_iota(jnp.int32, (PER, LANES), 1)
    token = lax.broadcasted_iota(jnp.int32, (PER, LANES), 0)
    spot = lax.rem(token, M)
    sequences = chunks * (PER // M)
    base = PER * lax.rem(place, LANES // PER)

    def column(row):
        return jnp.sum(jnp.where(lane == base + token, row, 0.0), axis=1, keepdims=True)

    square_d = column(square_rows[0:1] + square_rows[1:2])
    square_u = column(square_rows[2:3] + square_rows[3:4])
    scale_d = lax.rsqrt(square_d * inverse + EPS)
    scale_u = lax.rsqrt(square_u * inverse + EPS)
    down_lane = lane < R
    up_lane = jnp.logical_and(lane >= R, lane < 2 * R)
    low_lane = lane < 2 * R
    scale = jnp.where(down_lane, scale_d, scale_u)
    projected = jnp.where(low_lane, main, 0.0)
    pre = projected * scale
    sigma = jax.nn.sigmoid(pre)
    act = pre * sigma

    act_e = jnp.where(is_first, act[:, R : 2 * R], act[:, 0:R])
    cot_e = jnp.where(is_first, main[:, 3 * R :], main[:, 2 * R : 3 * R])
    own = jnp.concatenate([folded[:, R * r : R * r + R] for r in range(4)], axis=0)
    act_own = nn(act_e, own, HIGH)
    out_b = cot_e + act_own
    square_e = jnp.where(is_first, square_u, square_d)
    square_e = square_e + jnp.sum(act_e * (cot_e + out_b), axis=1, keepdims=True)
    scale_e = lax.rsqrt(jnp.maximum(square_e, 0.0) * inverse + EPS)
    raw = base_logits + nn(act_e, cross, HIGH)
    logits = raw * scale_e
    block = lax.div(place, LANES // PER)
    ids_d = down_ids[pl.ds(block, 1), :]
    ids_u = up_ids[pl.ds(block, 1), :]
    ids = jnp.where(is_first, ids_u, ids_d).astype(F32)
    group = lax.div(lane, R)
    within = lax.rem(lane, R)
    weight_sum = jnp.float32(0.0)
    for k in range(heads):
        weight_sum = weight_sum + loss_weights[k].astype(F32)
    top = jnp.zeros((PER, LANES), F32)
    target = jnp.zeros((PER, LANES), F32)
    weight = jnp.zeros((PER, LANES), F32)
    for k in range(heads):
        mine = group == k
        shift = offsets[k]
        largest = jnp.max(jnp.where(mine, logits, -jnp.inf), axis=1, keepdims=True)
        wanted = jnp.sum(jnp.where(lane == base + token + shift, ids, 0.0), axis=1, keepdims=True)
        factor = loss_weights[k].astype(F32) / weight_sum / ((M - shift) * sequences).astype(F32)
        valid = jnp.where(spot + shift < M, factor, 0.0)
        top = jnp.where(mine, largest, top)
        target = jnp.where(mine, wanted, target)
        weight = jnp.where(mine, valid, weight)
    power = jnp.exp(logits - top)
    below = jnp.ones((PER, LANES), F32)
    for k in range(heads):
        mine = group == k
        below = jnp.where(mine, jnp.sum(jnp.where(mine, power, 0.0), axis=1, keepdims=True), below)
    hit = jnp.where(within == target.astype(jnp.int32), 1.0, 0.0)
    per_lane = hit * (top + jnp.log(below) - logits) * weight
    loss = jnp.sum(jnp.sum(per_lane, axis=1, keepdims=True), axis=0, keepdims=True)
    grad = weight * (power / below - hit)
    grad_cols = grad * scale_e
    coef_e = jnp.sum(grad * raw, axis=1, keepdims=True) * scale_e * scale_e * scale_e * inverse
    dg_e = nt(grad_cols, cross, HIGH) - coef_e * out_b

    dg = pltpu.roll(main, 2 * R, axis=1)
    dg_wide = jnp.concatenate([dg_e] * 4, axis=1)
    replace = jnp.logical_or(jnp.logical_and(is_last, down_lane), jnp.logical_and(is_first, up_lane))
    dg = jnp.where(replace, dg_wide, dg)
    d_pre = jnp.where(low_lane, dg * sigma * (1.0 + pre * (1.0 - sigma)), 0.0)
    d_scaled = d_pre * scale
    moved = d_pre * projected
    coef_d = jnp.sum(jnp.where(down_lane, moved, 0.0), axis=1, keepdims=True)
    coef_u = jnp.sum(jnp.where(up_lane, moved, 0.0), axis=1, keepdims=True)
    coef_d = coef_d * scale_d * scale_d * scale_d * inverse
    coef_u = coef_u * scale_u * scale_u * scale_u * inverse
    both = jnp.where(low_lane, act, pltpu.roll(d_scaled, 2 * R, axis=1))
    head = jnp.where(is_end, grad_cols, 0.0)

    def parts_of(row):
        high = row.astype(BF16).astype(F32)
        low = (row - high).astype(BF16).astype(F32)
        return [high, low, row - high - low]

    rows = []
    for col in (coef_d, coef_u, coef_e):
        row = jnp.sum(jnp.where(lane == token, col, 0.0), axis=0, keepdims=True)
        rows += parts_of(row)[0:2]
    rows += parts_of(jnp.broadcast_to(jnp.where(is_end, loss, 0.0), (1, LANES)))
    rows += [jnp.zeros((7, LANES), F32)]
    chunk = jnp.concatenate([both, head, jnp.concatenate(rows, axis=0)], axis=0)
    out[...] = jnp.broadcast_to(chunk.astype(BF16)[None], out.shape)


def tokens_of(received, first):
    chunks = received.shape[0]
    return received[:, first : first + PER, :].reshape(chunks * PER, LANES)


def coefficient(received, row):
    chunks = received.shape[0]
    lane = lax.broadcasted_iota(jnp.int32, (PER, LANES), 1)
    token = lax.broadcasted_iota(jnp.int32, (PER, LANES), 0)
    cols = []
    for j in range(chunks):
        rows = received[j, CROSS:BACK_ROWS, :].astype(F32)
        both = rows[row : row + 1] + rows[row + 1 : row + 2]
        cols.append(jnp.sum(jnp.where(lane == token, both, 0.0), axis=1, keepdims=True))
    return jnp.concatenate(cols, axis=0)


def at_rows(weights, group):
    zero = jnp.zeros_like(weights)
    return jnp.concatenate([weights if k == group else zero for k in range(LANES // R)], axis=0)


def cotangent(received, side, x, c, w, gain, cand, end, cot):
    cot[...] = c[...].astype(F32)

    @pl.when(end)
    def _():
        high, low = halves(columns_of(gain, cand))
        grad = tokens_of(received, PER)
        final = x[...].astype(F32) + nn(tokens_of(received, 0), at_rows(w[R : 2 * R], side))
        cot[...] = nn(grad, high) + nn(grad, low) - coefficient(received, 4) * final


def weight_grads(meta, received, x_d, x_u, c_d, c_u, w_d, w_u, gain, cand, g_d, g_u, cot):
    is_first = meta[1] == 0
    is_last = meta[1] == meta[2] - 1
    act = tokens_of(received, 0)
    work = ((1, x_u, c_u, w_u, g_u, is_first), (0, x_d, c_d, w_d, g_d, is_last))
    for side, x, c, w, g, end in work:
        cotangent(received, side, x, c, w, gain, cand, end, cot)
        by_cot = tn(act, cot[...].astype(BF16))
        by_x = tn(act, x[...])
        grads = jnp.concatenate(
            [by_x[64 + R * side : 64 + R * side + R], by_cot[R * side : R * side + R]], axis=0
        )
        g[...] = grads.astype(g.dtype)


def token_grads(meta, received, x_d, x_u, c_d, c_u, w_d, w_u, gain, cand, ahead, behind, loss, cot):
    is_first = meta[1] == 0
    is_last = meta[1] == meta[2] - 1
    act = tokens_of(received, 0)
    work = (
        (1, x_u, c_u, w_u, behind.at[0], ahead.at[1], is_first),
        (0, x_d, c_d, w_d, ahead.at[0], behind.at[1], is_last),
    )
    for side, x, c, w, y, dx, end in work:
        wide = x[...].astype(F32)
        y[...] = (wide + nn(act, at_rows(w[R : 2 * R], side))).astype(BF16)
        cotangent(received, side, x, c, w, gain, cand, end, cot)
        back = cot[...] + nn(act, at_rows(w[0:R], 2 + side)) - coefficient(received, 2 * side) * wide
        dx[...] = back.astype(BF16)
    rows = jnp.sum(received[:, CROSS:BACK_ROWS, :].astype(F32), axis=0)
    total = rows[6:7] + rows[7:8] + rows[8:9]
    loss[...] = jnp.broadcast_to(total, loss.shape)


def finish(ahead, behind, g_d, mate, losses, down_next, up_next, down_back, up_back, grad_a, grad_b, loss, sems):
    copies = [
        pltpu.make_async_copy(ahead.at[0], down_next, sems.at[0]),
        pltpu.make_async_copy(behind.at[0], up_next, sems.at[1]),
        pltpu.make_async_copy(behind.at[1], down_back, sems.at[2]),
        pltpu.make_async_copy(ahead.at[1], up_back, sems.at[3]),
    ]
    for copy in copies:
        copy.start()
    total = g_d[...] + mate[...].astype(F32)
    grad_a[...] = total[0:R]
    grad_b[...] = total[R : 2 * R]
    loss[0] = jnp.sum(losses[:, 0:1])
    for copy in copies:
        copy.wait()


def shards(
    down_in,
    up_in,
    down_cot,
    up_cot,
    adapt_a,
    adapt_b,
    head_gain,
    cand,
    down_ids,
    up_ids,
    offsets,
    loss_weights,
):
    sections = lax.axis_size("section")
    groups = lax.axis_size("dp")
    position = lax.axis_index("section")
    place = lax.axis_index("dp")
    tokens, local_width = down_in.shape[1:]
    heads, candidates = head_gain.shape[0], cand.shape[0]
    mirror = [(i, sections - 1 - i) for i in range(sections)]
    further = [(i, i + 1) for i in range(sections - 1)]
    nearer = [(i + 1, i) for i in range(sections - 1)]
    smem = pl.BlockSpec(memory_space=pltpu.SMEM)
    vmem = pl.BlockSpec(memory_space=pltpu.VMEM)
    hbm = pl.BlockSpec(memory_space=pltpu.HBM)
    params = pltpu.CompilerParams(vmem_limit_bytes=48 << 20)
    shape = jax.ShapeDtypeStruct
    wide = shape((tokens, local_width), BF16)
    both = shape((2, tokens, local_width), BF16)

    w_d = pl.pallas_call(
        packed,
        out_shape=shape((2 * R, local_width), BF16),
        in_specs=[hbm] * 2,
        out_specs=vmem,
        scratch_shapes=[pltpu.SemaphoreType.DMA((2,))],
        compiler_params=params,
    )(in_hbm(adapt_a[0].T), in_hbm(adapt_b[0]))
    w_u = lax.ppermute(w_d, "section", mirror)
    sizes = jnp.int32(sections), jnp.int32(head_gain.shape[1])
    meta = jnp.stack([place.astype(jnp.int32), position.astype(jnp.int32), *sizes])
    meta = jnp.concatenate([meta, offsets, loss_weights])
    id_rows = (tokens // LANES, LANES)
    ids = down_ids.reshape(id_rows), up_ids.reshape(id_rows)
    fetched = (down_in[0], up_in[0], down_cot[0], up_cot[0], head_gain, cand, *ids)

    near = tokens // PER
    rings = [list(range(first, first + near)) for first in range(0, groups, near)]
    partners = [list(members) for members in zip(*rings)]
    send = shape((near, ROWS, LANES), BF16)
    partial, x_d, x_u, c_d, c_u, gain_part, cand_part, ids_d, ids_u = pl.pallas_call(
        first_partial,
        out_shape=(
            send,
            wide,
            wide,
            wide,
            wide,
            shape((heads, local_width), F32),
            shape((candidates, local_width), BF16),
            shape(id_rows, jnp.int32),
            shape(id_rows, jnp.int32),
        ),
        in_specs=[smem] + [hbm] * 8 + [vmem],
        out_specs=(vmem,) * 9,
        scratch_shapes=[pltpu.SemaphoreType.DMA((8,))],
        compiler_params=params,
    )(meta, *(in_hbm(held) for held in fetched), w_d)
    partial = pl.pallas_call(
        second_partial,
        out_shape=send,
        in_specs=[smem] + [vmem] * 7,
        out_specs=vmem,
        compiler_params=params,
    )(meta, partial, x_u, c_u, w_u, w_d, gain_part, cand_part)
    received = lax.all_to_all(partial, "dp", 0, 0, axis_index_groups=rings)
    summed = pl.pallas_call(
        gathered_sum,
        out_shape=shape((ROWS, LANES), BF16),
        in_specs=[vmem],
        out_specs=vmem,
        compiler_params=params,
    )(received)
    received = lax.all_gather(summed, "dp", axis_index_groups=partners)

    back = pl.pallas_call(
        middle,
        out_shape=shape((near, BACK_ROWS, LANES), BF16),
        in_specs=[smem] + [vmem] * 3,
        out_specs=vmem,
        compiler_params=params,
    )(meta, received, ids_d, ids_u)
    gathered = lax.all_to_all(back, "dp", 0, 0, axis_index_groups=rings)

    held = (meta, gathered, x_d, x_u, c_d, c_u, w_d, w_u, gain_part, cand_part)
    g_d, g_u = pl.pallas_call(
        weight_grads,
        out_shape=(shape((2 * R, local_width), F32), shape((2 * R, local_width), BF16)),
        in_specs=[smem] + [vmem] * 9,
        out_specs=(vmem,) * 2,
        scratch_shapes=[pltpu.VMEM((tokens, local_width), F32)],
        compiler_params=params,
    )(*held)
    mate = lax.ppermute(g_u, "section", mirror)
    ahead, behind, loss_rows = pl.pallas_call(
        token_grads,
        out_shape=(both, both, shape((sections, LANES), F32)),
        in_specs=[smem] + [vmem] * 9,
        out_specs=(vmem,) * 3,
        scratch_shapes=[pltpu.VMEM((tokens, local_width), F32)],
        compiler_params=params,
    )(*held)
    ahead = lax.ppermute(ahead, "section", further)
    behind = lax.ppermute(behind, "section", nearer)
    losses = lax.all_to_all(loss_rows, "section", 0, 0, tiled=True)
    down_next, up_next, down_back, up_back, grad_a, grad_b, loss = pl.pallas_call(
        finish,
        out_shape=(
            wide,
            wide,
            wide,
            wide,
            shape((R, local_width), F32),
            shape((R, local_width), F32),
            shape((1,), F32),
        ),
        in_specs=[vmem] * 5,
        out_specs=(hbm,) * 4 + (vmem, vmem, smem),
        scratch_shapes=[pltpu.SemaphoreType.DMA((4,))],
        compiler_params=params,
    )(ahead, behind, g_d, mate, losses)
    return (
        down_next[None],
        up_next[None],
        down_back[None],
        up_back[None],
        grad_a.T[None],
        grad_b[None],
        loss,
    )


def solution(mesh):
    in_specs = (
        P("section", None, "dp"),
        P("section", None, "dp"),
        P("section", None, "dp"),
        P("section", None, "dp"),
        P("section", "dp", None),
        P("section", None, "dp"),
        P(),
        P(),
        P(),
        P(),
        P(),
        P(),
    )
    out_specs = (
        P("section", None, "dp"),
        P("section", None, "dp"),
        P("section", None, "dp"),
        P("section", None, "dp"),
        P("section", "dp", None),
        P("section", None, "dp"),
        P(),
    )
    return jax.shard_map(shards, mesh=mesh, in_specs=in_specs, out_specs=out_specs, check_vma=False)
```

```python
import jax
import jax.numpy as jnp
from jax import lax
from jax.experimental import pallas as pl
from jax.experimental.pallas import tpu as pltpu
from jax.sharding import PartitionSpec as P

EPS = 1e-05
F32 = jnp.float32
BF16 = jnp.bfloat16
HIGH = lax.Precision.HIGHEST
R = 32
M = 32
LANES = 128
PER = 64
CROSS = 2 * PER
EXTRA = CROSS + R
ROWS = EXTRA + 16
BACK_ROWS = 2 * PER + 16


def nt(a, b, precision=None):
    return lax.dot_general(a, b, (((1,), (1,)), ((), ())), precision=precision, preferred_element_type=F32)


def nn(a, b, precision=None):
    return lax.dot_general(a, b, (((1,), (0,)), ((), ())), precision=precision, preferred_element_type=F32)


def tn(a, b):
    return lax.dot_general(a, b, (((0,), (0,)), ((), ())), preferred_element_type=F32)


def halves(value):
    high = value.astype(BF16)
    return high, (value - high.astype(F32)).astype(BF16)


def columns_of(gain_ref, cand_ref):
    cand = cand_ref[...].astype(F32)
    return jnp.concatenate([gain_ref[k : k + 1, :] * cand for k in range(gain_ref.shape[0])], axis=0)


def squares_row(block):
    wide = block.astype(F32)
    ones = jnp.ones((8, wide.shape[1]), BF16)
    high, low = halves(wide * wide)
    return (nt(ones, high) + nt(ones, low))[0:1, :]


def gated(weights, flag):
    return jnp.where(flag, weights.astype(F32), 0.0).astype(BF16)


def in_hbm(value):
    return pltpu.with_memory_space_constraint(value, pltpu.HBM)


def packed(a_hbm, b_hbm, w, sems):
    copies = [
        pltpu.make_async_copy(a_hbm, w.at[0:R], sems.at[0]),
        pltpu.make_async_copy(b_hbm, w.at[R : 2 * R], sems.at[1]),
    ]
    for copy in copies:
        copy.start()
    for copy in copies:
        copy.wait()


def first_partial(
    meta,
    x_d_hbm,
    x_u_hbm,
    c_d_hbm,
    c_u_hbm,
    gain_hbm,
    cand_hbm,
    ids_d_hbm,
    ids_u_hbm,
    w_d,
    out,
    x_d,
    x_u,
    c_d,
    c_u,
    gain,
    cand,
    ids_d,
    ids_u,
    sems,
):
    sections = meta[2]
    is_first = meta[1] == 0
    is_last = meta[1] == sections - 1
    chunks = out.shape[0]
    width = x_d.shape[1]
    here = pl.ds(pl.multiple_of(meta[0] * width, width), width)
    get_x_d = pltpu.make_async_copy(x_d_hbm, x_d, sems.at[0])
    get_c_d = pltpu.make_async_copy(c_d_hbm, c_d, sems.at[1])
    get_x_u = pltpu.make_async_copy(x_u_hbm, x_u, sems.at[2])
    get_c_u = pltpu.make_async_copy(c_u_hbm, c_u, sems.at[3])
    get_gain = pltpu.make_async_copy(gain_hbm.at[:, here], gain, sems.at[4])
    get_cand = pltpu.make_async_copy(cand_hbm.at[:, here], cand, sems.at[5])
    get_ids_d = pltpu.make_async_copy(ids_d_hbm, ids_d, sems.at[6])
    get_ids_u = pltpu.make_async_copy(ids_u_hbm, ids_u, sems.at[7])
    for copy in (get_x_d, get_c_d, get_x_u, get_gain, get_cand, get_c_u, get_ids_d, get_ids_u):
        copy.start()
    a_d, b_d = w_d[0:R], w_d[R : 2 * R]
    zero = jnp.zeros((R, width), BF16)
    wx = jnp.concatenate([a_d, zero, gated(b_d, is_last), zero], axis=0)
    wc = jnp.concatenate([zero, zero, gated(b_d, jnp.logical_not(is_last)), zero], axis=0)
    out[:, CROSS:EXTRA, :] = jnp.zeros((chunks, R, LANES), BF16)
    get_x_d.wait()
    get_c_d.wait()
    main = nt(x_d[...], wx) + nt(c_d[...], wc)
    out[:, 0:PER, :] = main.astype(BF16).reshape(chunks, PER, LANES)
    get_x_u.wait()
    rows = []
    for block in (x_d[...], x_u[...]):
        row = squares_row(block)
        high = row.astype(BF16).astype(F32)
        rows += [high, row - high]
    per = LANES // PER
    pad = jnp.zeros((8, LANES), F32)
    for j in range(chunks):
        start = (j // per) * LANES
        piece = [row[:, start : start + LANES] for row in rows]
        tail = jnp.concatenate([pad] + piece + [pad[0:4]], axis=0)
        out[j, EXTRA:ROWS, :] = tail.astype(BF16)
    get_gain.wait()
    get_cand.wait()

    def logits_of(block):
        high, low = halves(columns_of(gain, cand))
        value = nt(block, high) + nt(block, low)
        out[:, PER:CROSS, :] = value.astype(BF16).reshape(chunks, PER, LANES)

    @pl.when(is_last)
    def _():
        logits_of(x_d[...])

    @pl.when(is_first)
    def _():
        logits_of(x_u[...])

    @pl.when(jnp.logical_not(jnp.logical_or(is_first, is_last)))
    def _():
        out[:, PER:CROSS, :] = jnp.zeros((chunks, PER, LANES), BF16)

    get_c_u.wait()
    get_ids_d.wait()
    get_ids_u.wait()


def second_partial(meta, partial, x_u, c_u, w_u, w_d, gain, cand, out):
    is_first = meta[1] == 0
    is_last = meta[1] == meta[2] - 1
    chunks = out.shape[0]
    width = x_u.shape[1]
    a_u, b_u = w_u[0:R], w_u[R : 2 * R]
    zero = jnp.zeros((R, width), BF16)
    wx = jnp.concatenate([zero, a_u, zero, gated(b_u, is_first)], axis=0)
    wc = jnp.concatenate([zero, zero, zero, gated(b_u, jnp.logical_not(is_first))], axis=0)
    main = nt(x_u[...], wx) + nt(c_u[...], wc)
    main = main.reshape(chunks, PER, LANES) + partial[:, 0:PER, :].astype(F32)
    out[:, 0:PER, :] = main.astype(BF16)
    out[:, PER:ROWS, :] = partial[:, PER:ROWS, :]

    @pl.when(jnp.logical_or(is_first, is_last))
    def _():
        b_d = w_d[R : 2 * R]
        b_e = jnp.where(is_last, b_d.astype(F32), b_u.astype(F32)).astype(BF16)
        high, low = halves(columns_of(gain, cand))
        cross = nt(b_e, high) + nt(b_e, low)
        own = nt(b_e, b_e)
        folded = jnp.concatenate([own[8 * r : 8 * r + 8] for r in range(4)], axis=1)
        tail = jnp.concatenate([folded, jnp.zeros((8, LANES), F32)], axis=0)
        out[:, CROSS:EXTRA, :] = jnp.broadcast_to(cross.astype(BF16)[None], (chunks, R, LANES))
        held = partial[:, EXTRA:ROWS, :].astype(F32) + tail[None]
        out[:, EXTRA:ROWS, :] = held.astype(BF16)


def gathered_sum(received, out):
    total = jnp.sum(received[...].astype(F32), axis=0)
    folded = total[EXTRA : EXTRA + 8]
    rows = [folded]
    for side in range(2):
        first = EXTRA + 8 + 2 * side
        row = total[first : first + 1] + total[first + 1 : first + 2]
        high = row.astype(BF16).astype(F32)
        rows += [high, row - high]
    rows += [jnp.zeros((4, LANES), F32)]
    out[0:EXTRA] = total[0:EXTRA].astype(BF16)
    out[EXTRA:ROWS] = jnp.concatenate(rows, axis=0).astype(BF16)


def middle(meta, received, down_ids, up_ids, out):
    chunks = out.shape[0]
    place = lax.rem(meta[0], chunks)
    is_first = meta[1] == 0
    is_last = meta[1] == meta[2] - 1
    is_end = jnp.logical_or(is_first, is_last)
    inverse = 1.0 / meta[3].astype(F32)
    heads = LANES // R
    offsets = [meta[4 + k] for k in range(heads)]
    loss_weights = [meta[4 + heads + k] for k in range(heads)]
    total = received[0].astype(F32) + received[1].astype(F32)
    main, base_logits, cross = total[0:PER], total[PER:CROSS], total[CROSS:EXTRA]
    folded, square_rows = total[EXTRA : EXTRA + 8], total[EXTRA + 8 : EXTRA + 12]
    lane = lax.broadcasted_iota(jnp.int32, (PER, LANES), 1)
    token = lax.broadcasted_iota(jnp.int32, (PER, LANES), 0)
    spot = lax.rem(token, M)
    sequences = chunks * (PER // M)
    base = PER * lax.rem(place, LANES // PER)

    def column(row):
        return jnp.sum(jnp.where(lane == base + token, row, 0.0), axis=1, keepdims=True)

    square_d = column(square_rows[0:1] + square_rows[1:2])
    square_u = column(square_rows[2:3] + square_rows[3:4])
    scale_d = lax.rsqrt(square_d * inverse + EPS)
    scale_u = lax.rsqrt(square_u * inverse + EPS)
    down_lane = lane < R
    up_lane = jnp.logical_and(lane >= R, lane < 2 * R)
    low_lane = lane < 2 * R
    scale = jnp.where(down_lane, scale_d, scale_u)
    projected = jnp.where(low_lane, main, 0.0)
    pre = projected * scale
    sigma = jax.nn.sigmoid(pre)
    act = pre * sigma

    act_e = jnp.where(is_first, act[:, R : 2 * R], act[:, 0:R])
    cot_e = jnp.where(is_first, main[:, 3 * R :], main[:, 2 * R : 3 * R])
    own = jnp.concatenate([folded[:, R * r : R * r + R] for r in range(4)], axis=0)
    act_own = nn(act_e, own, HIGH)
    out_b = cot_e + act_own
    square_e = jnp.where(is_first, square_u, square_d)
    square_e = square_e + jnp.sum(act_e * (cot_e + out_b), axis=1, keepdims=True)
    scale_e = lax.rsqrt(jnp.maximum(square_e, 0.0) * inverse + EPS)
    raw = base_logits + nn(act_e, cross, HIGH)
    logits = raw * scale_e
    block = lax.div(place, LANES // PER)
    ids_d = down_ids[pl.ds(block, 1), :]
    ids_u = up_ids[pl.ds(block, 1), :]
    ids = jnp.where(is_first, ids_u, ids_d).astype(F32)
    group = lax.div(lane, R)
    within = lax.rem(lane, R)
    weight_sum = jnp.float32(0.0)
    for k in range(heads):
        weight_sum = weight_sum + loss_weights[k].astype(F32)
    top = jnp.zeros((PER, LANES), F32)
    target = jnp.zeros((PER, LANES), F32)
    weight = jnp.zeros((PER, LANES), F32)
    for k in range(heads):
        mine = group == k
        shift = offsets[k]
        largest = jnp.max(jnp.where(mine, logits, -jnp.inf), axis=1, keepdims=True)
        wanted = jnp.sum(jnp.where(lane == base + token + shift, ids, 0.0), axis=1, keepdims=True)
        factor = loss_weights[k].astype(F32) / weight_sum / ((M - shift) * sequences).astype(F32)
        valid = jnp.where(spot + shift < M, factor, 0.0)
        top = jnp.where(mine, largest, top)
        target = jnp.where(mine, wanted, target)
        weight = jnp.where(mine, valid, weight)
    power = jnp.exp(logits - top)
    below = jnp.ones((PER, LANES), F32)
    for k in range(heads):
        mine = group == k
        below = jnp.where(mine, jnp.sum(jnp.where(mine, power, 0.0), axis=1, keepdims=True), below)
    hit = jnp.where(within == target.astype(jnp.int32), 1.0, 0.0)
    per_lane = hit * (top + jnp.log(below) - logits) * weight
    loss = jnp.sum(jnp.sum(per_lane, axis=1, keepdims=True), axis=0, keepdims=True)
    grad = weight * (power / below - hit)
    grad_cols = grad * scale_e
    coef_e = jnp.sum(grad * raw, axis=1, keepdims=True) * scale_e * scale_e * scale_e * inverse
    dg_e = nt(grad_cols, cross, HIGH) - coef_e * out_b

    dg = pltpu.roll(main, 2 * R, axis=1)
    dg_wide = jnp.concatenate([dg_e] * 4, axis=1)
    replace = jnp.logical_or(jnp.logical_and(is_last, down_lane), jnp.logical_and(is_first, up_lane))
    dg = jnp.where(replace, dg_wide, dg)
    d_pre = jnp.where(low_lane, dg * sigma * (1.0 + pre * (1.0 - sigma)), 0.0)
    d_scaled = d_pre * scale
    moved = d_pre * projected
    coef_d = jnp.sum(jnp.where(down_lane, moved, 0.0), axis=1, keepdims=True)
    coef_u = jnp.sum(jnp.where(up_lane, moved, 0.0), axis=1, keepdims=True)
    coef_d = coef_d * scale_d * scale_d * scale_d * inverse
    coef_u = coef_u * scale_u * scale_u * scale_u * inverse
    both = jnp.where(low_lane, act, pltpu.roll(d_scaled, 2 * R, axis=1))
    head = jnp.where(is_end, grad_cols, 0.0)

    def parts_of(row):
        high = row.astype(BF16).astype(F32)
        low = (row - high).astype(BF16).astype(F32)
        return [high, low, row - high - low]

    rows = []
    for col in (coef_d, coef_u, coef_e):
        row = jnp.sum(jnp.where(lane == token, col, 0.0), axis=0, keepdims=True)
        rows += parts_of(row)[0:2]
    rows += parts_of(jnp.broadcast_to(jnp.where(is_end, loss, 0.0), (1, LANES)))
    rows += [jnp.zeros((7, LANES), F32)]
    chunk = jnp.concatenate([both, head, jnp.concatenate(rows, axis=0)], axis=0)
    out[...] = jnp.broadcast_to(chunk.astype(BF16)[None], out.shape)


def tokens_of(received, first):
    chunks = received.shape[0]
    return received[:, first : first + PER, :].reshape(chunks * PER, LANES)


def coefficient(received, row):
    chunks = received.shape[0]
    lane = lax.broadcasted_iota(jnp.int32, (PER, LANES), 1)
    token = lax.broadcasted_iota(jnp.int32, (PER, LANES), 0)
    cols = []
    for j in range(chunks):
        rows = received[j, CROSS:BACK_ROWS, :].astype(F32)
        both = rows[row : row + 1] + rows[row + 1 : row + 2]
        cols.append(jnp.sum(jnp.where(lane == token, both, 0.0), axis=1, keepdims=True))
    return jnp.concatenate(cols, axis=0)


def at_rows(weights, group):
    zero = jnp.zeros_like(weights)
    return jnp.concatenate([weights if k == group else zero for k in range(LANES // R)], axis=0)


def cotangent(received, side, x, c, w, gain, cand, end, cot):
    cot[...] = c[...].astype(F32)

    @pl.when(end)
    def _():
        high, low = halves(columns_of(gain, cand))
        grad = tokens_of(received, PER)
        final = x[...].astype(F32) + nn(tokens_of(received, 0), at_rows(w[R : 2 * R], side))
        cot[...] = nn(grad, high) + nn(grad, low) - coefficient(received, 4) * final


def weight_grads(meta, received, x_d, x_u, c_d, c_u, w_d, w_u, gain, cand, g_d, g_u, cot):
    is_first = meta[1] == 0
    is_last = meta[1] == meta[2] - 1
    act = tokens_of(received, 0)
    work = ((1, x_u, c_u, w_u, g_u, is_first), (0, x_d, c_d, w_d, g_d, is_last))
    for side, x, c, w, g, end in work:
        cotangent(received, side, x, c, w, gain, cand, end, cot)
        by_cot = tn(act, cot[...].astype(BF16))
        by_x = tn(act, x[...])
        grads = jnp.concatenate(
            [by_x[64 + R * side : 64 + R * side + R], by_cot[R * side : R * side + R]], axis=0
        )
        g[...] = grads.astype(g.dtype)


def token_grads(meta, received, x_d, x_u, c_d, c_u, w_d, w_u, gain, cand, outer, inner, loss, cot):
    is_first = meta[1] == 0
    is_last = meta[1] == meta[2] - 1
    is_even = lax.rem(meta[1], 2) == 0

    def fill(ahead, behind):
        act = tokens_of(received, 0)
        work = (
            (1, x_u, c_u, w_u, behind.at[0], ahead.at[1], is_first),
            (0, x_d, c_d, w_d, ahead.at[0], behind.at[1], is_last),
        )
        for side, x, c, w, y, dx, end in work:
            wide = x[...].astype(F32)
            y[...] = (wide + nn(act, at_rows(w[R : 2 * R], side))).astype(BF16)
            cotangent(received, side, x, c, w, gain, cand, end, cot)
            back = cot[...] + nn(act, at_rows(w[0:R], 2 + side)) - coefficient(received, 2 * side) * wide
            dx[...] = back.astype(BF16)

    @pl.when(is_even)
    def _():
        fill(inner, outer)

    @pl.when(jnp.logical_not(is_even))
    def _():
        fill(outer, inner)

    rows = jnp.sum(received[:, CROSS:BACK_ROWS, :].astype(F32), axis=0)
    total = rows[6:7] + rows[7:8] + rows[8:9]
    loss[...] = jnp.broadcast_to(total, loss.shape)


def finish(
    meta, outer, inner, g_d, mate, losses, down_next, up_next, down_back, up_back, grad_a, grad_b, loss, sems
):
    is_even = lax.rem(meta[1], 2) == 0
    total = g_d[...] + mate[...].astype(F32)
    grad_a[...] = total[0:R]
    grad_b[...] = total[R : 2 * R]
    loss[0] = jnp.sum(losses[:, 0:1])

    def write(ahead, behind):
        copies = [
            pltpu.make_async_copy(ahead.at[0], down_next, sems.at[0]),
            pltpu.make_async_copy(behind.at[0], up_next, sems.at[1]),
            pltpu.make_async_copy(behind.at[1], down_back, sems.at[2]),
            pltpu.make_async_copy(ahead.at[1], up_back, sems.at[3]),
        ]
        for copy in copies:
            copy.start()
        for copy in copies:
            copy.wait()

    @pl.when(is_even)
    def _():
        write(outer, inner)

    @pl.when(jnp.logical_not(is_even))
    def _():
        write(inner, outer)


def shards(
    down_in,
    up_in,
    down_cot,
    up_cot,
    adapt_a,
    adapt_b,
    head_gain,
    cand,
    down_ids,
    up_ids,
    offsets,
    loss_weights,
):
    sections = lax.axis_size("section")
    groups = lax.axis_size("dp")
    position = lax.axis_index("section")
    place = lax.axis_index("dp")
    tokens, local_width = down_in.shape[1:]
    heads, candidates = head_gain.shape[0], cand.shape[0]
    mirror = [(i, sections - 1 - i) for i in range(sections)]
    inside = [(i, i ^ 1) for i in range(sections)]
    between = [(i, i + 1 if i % 2 else i - 1) for i in range(1, sections - 1)]
    smem = pl.BlockSpec(memory_space=pltpu.SMEM)
    vmem = pl.BlockSpec(memory_space=pltpu.VMEM)
    hbm = pl.BlockSpec(memory_space=pltpu.HBM)
    params = pltpu.CompilerParams(vmem_limit_bytes=48 << 20)
    shape = jax.ShapeDtypeStruct
    wide = shape((tokens, local_width), BF16)
    both = shape((2, tokens, local_width), BF16)

    w_d = pl.pallas_call(
        packed,
        out_shape=shape((2 * R, local_width), BF16),
        in_specs=[hbm] * 2,
        out_specs=vmem,
        scratch_shapes=[pltpu.SemaphoreType.DMA((2,))],
        compiler_params=params,
    )(in_hbm(adapt_a[0].T), in_hbm(adapt_b[0]))
    w_u = lax.ppermute(w_d, "section", mirror)
    sizes = jnp.int32(sections), jnp.int32(head_gain.shape[1])
    meta = jnp.stack([place.astype(jnp.int32), position.astype(jnp.int32), *sizes])
    meta = jnp.concatenate([meta, offsets, loss_weights])
    id_rows = (tokens // LANES, LANES)
    ids = down_ids.reshape(id_rows), up_ids.reshape(id_rows)
    fetched = (down_in[0], up_in[0], down_cot[0], up_cot[0], head_gain, cand, *ids)

    near = tokens // PER
    rings = [list(range(first, first + near)) for first in range(0, groups, near)]
    partners = [list(members) for members in zip(*rings)]
    send = shape((near, ROWS, LANES), BF16)
    partial, x_d, x_u, c_d, c_u, gain_part, cand_part, ids_d, ids_u = pl.pallas_call(
        first_partial,
        out_shape=(
            send,
            wide,
            wide,
            wide,
            wide,
            shape((heads, local_width), F32),
            shape((candidates, local_width), BF16),
            shape(id_rows, jnp.int32),
            shape(id_rows, jnp.int32),
        ),
        in_specs=[smem] + [hbm] * 8 + [vmem],
        out_specs=(vmem,) * 9,
        scratch_shapes=[pltpu.SemaphoreType.DMA((8,))],
        compiler_params=params,
    )(meta, *(in_hbm(held) for held in fetched), w_d)
    partial = pl.pallas_call(
        second_partial,
        out_shape=send,
        in_specs=[smem] + [vmem] * 7,
        out_specs=vmem,
        compiler_params=params,
    )(meta, partial, x_u, c_u, w_u, w_d, gain_part, cand_part)
    received = lax.all_to_all(partial, "dp", 0, 0, axis_index_groups=rings)
    summed = pl.pallas_call(
        gathered_sum,
        out_shape=shape((ROWS, LANES), BF16),
        in_specs=[vmem],
        out_specs=vmem,
        compiler_params=params,
    )(received)
    received = lax.all_gather(summed, "dp", axis_index_groups=partners)

    back = pl.pallas_call(
        middle,
        out_shape=shape((near, BACK_ROWS, LANES), BF16),
        in_specs=[smem] + [vmem] * 3,
        out_specs=vmem,
        compiler_params=params,
    )(meta, received, ids_d, ids_u)
    gathered = lax.all_to_all(back, "dp", 0, 0, axis_index_groups=rings)

    held = (meta, gathered, x_d, x_u, c_d, c_u, w_d, w_u, gain_part, cand_part)
    g_d, g_u = pl.pallas_call(
        weight_grads,
        out_shape=(shape((2 * R, local_width), F32), shape((2 * R, local_width), BF16)),
        in_specs=[smem] + [vmem] * 9,
        out_specs=(vmem,) * 2,
        scratch_shapes=[pltpu.VMEM((tokens, local_width), F32)],
        compiler_params=params,
    )(*held)
    mate = lax.ppermute(g_u, "section", mirror)
    outer, inner, loss_rows = pl.pallas_call(
        token_grads,
        out_shape=(both, both, shape((sections, LANES), F32)),
        in_specs=[smem] + [vmem] * 9,
        out_specs=(vmem,) * 3,
        scratch_shapes=[pltpu.VMEM((tokens, local_width), F32)],
        compiler_params=params,
    )(*held)
    outer = lax.ppermute(outer, "section", between)
    inner = lax.ppermute(inner, "section", inside)
    losses = lax.all_to_all(loss_rows, "section", 0, 0, tiled=True)
    down_next, up_next, down_back, up_back, grad_a, grad_b, loss = pl.pallas_call(
        finish,
        out_shape=(
            wide,
            wide,
            wide,
            wide,
            shape((R, local_width), F32),
            shape((R, local_width), F32),
            shape((1,), F32),
        ),
        in_specs=[smem] + [vmem] * 5,
        out_specs=(hbm,) * 4 + (vmem, vmem, smem),
        scratch_shapes=[pltpu.SemaphoreType.DMA((4,))],
        compiler_params=params,
    )(meta, outer, inner, g_d, mate, losses)
    return (
        down_next[None],
        up_next[None],
        down_back[None],
        up_back[None],
        grad_a.T[None],
        grad_b[None],
        loss,
    )


def solution(mesh):
    in_specs = (
        P("section", None, "dp"),
        P("section", None, "dp"),
        P("section", None, "dp"),
        P("section", None, "dp"),
        P("section", "dp", None),
        P("section", None, "dp"),
        P(),
        P(),
        P(),
        P(),
        P(),
        P(),
    )
    out_specs = (
        P("section", None, "dp"),
        P("section", None, "dp"),
        P("section", None, "dp"),
        P("section", None, "dp"),
        P("section", "dp", None),
        P("section", None, "dp"),
        P(),
    )
    return jax.shard_map(shards, mesh=mesh, in_specs=in_specs, out_specs=out_specs, check_vma=False)
```

```python
import jax
import jax.numpy as jnp
from jax import lax
from jax.experimental import pallas as pl
from jax.experimental.pallas import tpu as pltpu
from jax.sharding import PartitionSpec as P

EPS = 1e-05
F32 = jnp.float32
BF16 = jnp.bfloat16
HIGH = lax.Precision.HIGHEST
R = 32
M = 32
LANES = 128
PER = 64
CROSS = 2 * PER
EXTRA = CROSS + R
ROWS = EXTRA + 16
BACK_ROWS = 2 * PER + 16


def nt(a, b, precision=None):
    return lax.dot_general(a, b, (((1,), (1,)), ((), ())), precision=precision, preferred_element_type=F32)


def nn(a, b, precision=None):
    return lax.dot_general(a, b, (((1,), (0,)), ((), ())), precision=precision, preferred_element_type=F32)


def tn(a, b):
    return lax.dot_general(a, b, (((0,), (0,)), ((), ())), preferred_element_type=F32)


def halves(value):
    high = value.astype(BF16)
    return high, (value - high.astype(F32)).astype(BF16)


def columns_of(gain_ref, cand_ref):
    cand = cand_ref[...].astype(F32)
    return jnp.concatenate([gain_ref[k : k + 1, :] * cand for k in range(gain_ref.shape[0])], axis=0)


def squares_row(block):
    wide = block.astype(F32)
    ones = jnp.ones((8, wide.shape[1]), BF16)
    high, low = halves(wide * wide)
    return (nt(ones, high) + nt(ones, low))[0:1, :]


def gated(weights, flag):
    return jnp.where(flag, weights.astype(F32), 0.0).astype(BF16)


def in_hbm(value):
    return pltpu.with_memory_space_constraint(value, pltpu.HBM)


def packed(a_hbm, b_hbm, w, sems):
    copies = [
        pltpu.make_async_copy(a_hbm, w.at[0:R], sems.at[0]),
        pltpu.make_async_copy(b_hbm, w.at[R : 2 * R], sems.at[1]),
    ]
    for copy in copies:
        copy.start()
    for copy in copies:
        copy.wait()


def first_partial(
    meta,
    x_d_hbm,
    x_u_hbm,
    c_d_hbm,
    c_u_hbm,
    gain_hbm,
    cand_hbm,
    ids_d_hbm,
    ids_u_hbm,
    offsets_hbm,
    weights_hbm,
    w_d,
    out,
    x_d,
    x_u,
    c_d,
    c_u,
    gain,
    cand,
    ids_d,
    ids_u,
    offsets,
    weights,
    sems,
):
    sections = meta[2]
    is_first = meta[1] == 0
    is_last = meta[1] == sections - 1
    chunks = out.shape[0]
    width = x_d.shape[1]
    here = pl.ds(pl.multiple_of(meta[0] * width, width), width)
    get_x_d = pltpu.make_async_copy(x_d_hbm, x_d, sems.at[0])
    get_c_d = pltpu.make_async_copy(c_d_hbm, c_d, sems.at[1])
    get_x_u = pltpu.make_async_copy(x_u_hbm, x_u, sems.at[2])
    get_c_u = pltpu.make_async_copy(c_u_hbm, c_u, sems.at[3])
    get_gain = pltpu.make_async_copy(gain_hbm.at[:, here], gain, sems.at[4])
    get_cand = pltpu.make_async_copy(cand_hbm.at[:, here], cand, sems.at[5])
    get_ids_d = pltpu.make_async_copy(ids_d_hbm, ids_d, sems.at[6])
    get_ids_u = pltpu.make_async_copy(ids_u_hbm, ids_u, sems.at[7])
    get_offsets = pltpu.make_async_copy(offsets_hbm, offsets, sems.at[8])
    get_weights = pltpu.make_async_copy(weights_hbm, weights, sems.at[9])
    small = (get_ids_d, get_ids_u, get_offsets, get_weights)
    for copy in (get_x_d, get_c_d, get_x_u, get_gain, get_cand, get_c_u, *small):
        copy.start()
    a_d, b_d = w_d[0:R], w_d[R : 2 * R]
    zero = jnp.zeros((R, width), BF16)
    wx = jnp.concatenate([a_d, zero, gated(b_d, is_last), zero], axis=0)
    wc = jnp.concatenate([zero, zero, gated(b_d, jnp.logical_not(is_last)), zero], axis=0)
    out[:, CROSS:EXTRA, :] = jnp.zeros((chunks, R, LANES), BF16)
    get_x_d.wait()
    get_c_d.wait()
    main = nt(x_d[...], wx) + nt(c_d[...], wc)
    out[:, 0:PER, :] = main.astype(BF16).reshape(chunks, PER, LANES)
    get_x_u.wait()
    rows = []
    for block in (x_d[...], x_u[...]):
        row = squares_row(block)
        high = row.astype(BF16).astype(F32)
        rows += [high, row - high]
    per = LANES // PER
    pad = jnp.zeros((8, LANES), F32)
    for j in range(chunks):
        start = (j // per) * LANES
        piece = [row[:, start : start + LANES] for row in rows]
        tail = jnp.concatenate([pad] + piece + [pad[0:4]], axis=0)
        out[j, EXTRA:ROWS, :] = tail.astype(BF16)
    get_gain.wait()
    get_cand.wait()

    def logits_of(block):
        high, low = halves(columns_of(gain, cand))
        value = nt(block, high) + nt(block, low)
        out[:, PER:CROSS, :] = value.astype(BF16).reshape(chunks, PER, LANES)

    @pl.when(is_last)
    def _():
        logits_of(x_d[...])

    @pl.when(is_first)
    def _():
        logits_of(x_u[...])

    @pl.when(jnp.logical_not(jnp.logical_or(is_first, is_last)))
    def _():
        out[:, PER:CROSS, :] = jnp.zeros((chunks, PER, LANES), BF16)

    get_c_u.wait()
    for copy in small:
        copy.wait()


def second_partial(meta, partial, x_u, c_u, w_u, w_d, gain, cand, out):
    is_first = meta[1] == 0
    is_last = meta[1] == meta[2] - 1
    chunks = out.shape[0]
    width = x_u.shape[1]
    a_u, b_u = w_u[0:R], w_u[R : 2 * R]
    zero = jnp.zeros((R, width), BF16)
    wx = jnp.concatenate([zero, a_u, zero, gated(b_u, is_first)], axis=0)
    wc = jnp.concatenate([zero, zero, zero, gated(b_u, jnp.logical_not(is_first))], axis=0)
    main = nt(x_u[...], wx) + nt(c_u[...], wc)
    main = main.reshape(chunks, PER, LANES) + partial[:, 0:PER, :].astype(F32)
    out[:, 0:PER, :] = main.astype(BF16)
    out[:, PER:ROWS, :] = partial[:, PER:ROWS, :]

    @pl.when(jnp.logical_or(is_first, is_last))
    def _():
        b_d = w_d[R : 2 * R]
        b_e = jnp.where(is_last, b_d.astype(F32), b_u.astype(F32)).astype(BF16)
        high, low = halves(columns_of(gain, cand))
        cross = nt(b_e, high) + nt(b_e, low)
        own = nt(b_e, b_e)
        folded = jnp.concatenate([own[8 * r : 8 * r + 8] for r in range(4)], axis=1)
        tail = jnp.concatenate([folded, jnp.zeros((8, LANES), F32)], axis=0)
        out[:, CROSS:EXTRA, :] = jnp.broadcast_to(cross.astype(BF16)[None], (chunks, R, LANES))
        held = partial[:, EXTRA:ROWS, :].astype(F32) + tail[None]
        out[:, EXTRA:ROWS, :] = held.astype(BF16)


def gathered_sum(received, out):
    total = jnp.sum(received[...].astype(F32), axis=0)
    folded = total[EXTRA : EXTRA + 8]
    rows = [folded]
    for side in range(2):
        first = EXTRA + 8 + 2 * side
        row = total[first : first + 1] + total[first + 1 : first + 2]
        high = row.astype(BF16).astype(F32)
        rows += [high, row - high]
    rows += [jnp.zeros((4, LANES), F32)]
    out[0:EXTRA] = total[0:EXTRA].astype(BF16)
    out[EXTRA:ROWS] = jnp.concatenate(rows, axis=0).astype(BF16)


def middle(meta, offsets, loss_weights, received, down_ids, up_ids, out):
    chunks = out.shape[0]
    place = lax.rem(meta[0], chunks)
    is_first = meta[1] == 0
    is_last = meta[1] == meta[2] - 1
    is_end = jnp.logical_or(is_first, is_last)
    inverse = 1.0 / meta[3].astype(F32)
    heads = LANES // R
    total = received[0].astype(F32) + received[1].astype(F32)
    main, base_logits, cross = total[0:PER], total[PER:CROSS], total[CROSS:EXTRA]
    folded, square_rows = total[EXTRA : EXTRA + 8], total[EXTRA + 8 : EXTRA + 12]
    lane = lax.broadcasted_iota(jnp.int32, (PER, LANES), 1)
    token = lax.broadcasted_iota(jnp.int32, (PER, LANES), 0)
    spot = lax.rem(token, M)
    sequences = chunks * (PER // M)
    base = PER * lax.rem(place, LANES // PER)

    def column(row):
        return jnp.sum(jnp.where(lane == base + token, row, 0.0), axis=1, keepdims=True)

    square_d = column(square_rows[0:1] + square_rows[1:2])
    square_u = column(square_rows[2:3] + square_rows[3:4])
    scale_d = lax.rsqrt(square_d * inverse + EPS)
    scale_u = lax.rsqrt(square_u * inverse + EPS)
    down_lane = lane < R
    up_lane = jnp.logical_and(lane >= R, lane < 2 * R)
    low_lane = lane < 2 * R
    scale = jnp.where(down_lane, scale_d, scale_u)
    projected = jnp.where(low_lane, main, 0.0)
    pre = projected * scale
    sigma = jax.nn.sigmoid(pre)
    act = pre * sigma

    act_e = jnp.where(is_first, act[:, R : 2 * R], act[:, 0:R])
    cot_e = jnp.where(is_first, main[:, 3 * R :], main[:, 2 * R : 3 * R])
    own = jnp.concatenate([folded[:, R * r : R * r + R] for r in range(4)], axis=0)
    act_own = nn(act_e, own, HIGH)
    out_b = cot_e + act_own
    square_e = jnp.where(is_first, square_u, square_d)
    square_e = square_e + jnp.sum(act_e * (cot_e + out_b), axis=1, keepdims=True)
    scale_e = lax.rsqrt(jnp.maximum(square_e, 0.0) * inverse + EPS)
    raw = base_logits + nn(act_e, cross, HIGH)
    logits = raw * scale_e
    block = lax.div(place, LANES // PER)
    ids_d = down_ids[pl.ds(block, 1), :]
    ids_u = up_ids[pl.ds(block, 1), :]
    ids = jnp.where(is_first, ids_u, ids_d).astype(F32)
    group = lax.div(lane, R)
    within = lax.rem(lane, R)
    weight_sum = jnp.float32(0.0)
    for k in range(heads):
        weight_sum = weight_sum + loss_weights[k].astype(F32)
    top = jnp.zeros((PER, LANES), F32)
    target = jnp.zeros((PER, LANES), F32)
    weight = jnp.zeros((PER, LANES), F32)
    for k in range(heads):
        mine = group == k
        shift = offsets[k]
        largest = jnp.max(jnp.where(mine, logits, -jnp.inf), axis=1, keepdims=True)
        wanted = jnp.sum(jnp.where(lane == base + token + shift, ids, 0.0), axis=1, keepdims=True)
        factor = loss_weights[k].astype(F32) / weight_sum / ((M - shift) * sequences).astype(F32)
        valid = jnp.where(spot + shift < M, factor, 0.0)
        top = jnp.where(mine, largest, top)
        target = jnp.where(mine, wanted, target)
        weight = jnp.where(mine, valid, weight)
    power = jnp.exp(logits - top)
    below = jnp.ones((PER, LANES), F32)
    for k in range(heads):
        mine = group == k
        below = jnp.where(mine, jnp.sum(jnp.where(mine, power, 0.0), axis=1, keepdims=True), below)
    hit = jnp.where(within == target.astype(jnp.int32), 1.0, 0.0)
    per_lane = hit * (top + jnp.log(below) - logits) * weight
    loss = jnp.sum(jnp.sum(per_lane, axis=1, keepdims=True), axis=0, keepdims=True)
    grad = weight * (power / below - hit)
    grad_cols = grad * scale_e
    coef_e = jnp.sum(grad * raw, axis=1, keepdims=True) * scale_e * scale_e * scale_e * inverse
    dg_e = nt(grad_cols, cross, HIGH) - coef_e * out_b

    dg = pltpu.roll(main, 2 * R, axis=1)
    dg_wide = jnp.concatenate([dg_e] * 4, axis=1)
    replace = jnp.logical_or(jnp.logical_and(is_last, down_lane), jnp.logical_and(is_first, up_lane))
    dg = jnp.where(replace, dg_wide, dg)
    d_pre = jnp.where(low_lane, dg * sigma * (1.0 + pre * (1.0 - sigma)), 0.0)
    d_scaled = d_pre * scale
    moved = d_pre * projected
    coef_d = jnp.sum(jnp.where(down_lane, moved, 0.0), axis=1, keepdims=True)
    coef_u = jnp.sum(jnp.where(up_lane, moved, 0.0), axis=1, keepdims=True)
    coef_d = coef_d * scale_d * scale_d * scale_d * inverse
    coef_u = coef_u * scale_u * scale_u * scale_u * inverse
    both = jnp.where(low_lane, act, pltpu.roll(d_scaled, 2 * R, axis=1))
    head = jnp.where(is_end, grad_cols, 0.0)

    def parts_of(row):
        high = row.astype(BF16).astype(F32)
        low = (row - high).astype(BF16).astype(F32)
        return [high, low, row - high - low]

    rows = []
    for col in (coef_d, coef_u, coef_e):
        row = jnp.sum(jnp.where(lane == token, col, 0.0), axis=0, keepdims=True)
        rows += parts_of(row)[0:2]
    rows += parts_of(jnp.broadcast_to(jnp.where(is_end, loss, 0.0), (1, LANES)))
    rows += [jnp.zeros((7, LANES), F32)]
    chunk = jnp.concatenate([both, head, jnp.concatenate(rows, axis=0)], axis=0)
    out[...] = jnp.broadcast_to(chunk.astype(BF16)[None], out.shape)


def tokens_of(received, first):
    chunks = received.shape[0]
    return received[:, first : first + PER, :].reshape(chunks * PER, LANES)


def coefficient(received, row):
    chunks = received.shape[0]
    lane = lax.broadcasted_iota(jnp.int32, (PER, LANES), 1)
    token = lax.broadcasted_iota(jnp.int32, (PER, LANES), 0)
    cols = []
    for j in range(chunks):
        rows = received[j, CROSS:BACK_ROWS, :].astype(F32)
        both = rows[row : row + 1] + rows[row + 1 : row + 2]
        cols.append(jnp.sum(jnp.where(lane == token, both, 0.0), axis=1, keepdims=True))
    return jnp.concatenate(cols, axis=0)


def at_rows(weights, group):
    zero = jnp.zeros_like(weights)
    return jnp.concatenate([weights if k == group else zero for k in range(LANES // R)], axis=0)


def backward(meta, received, x_d, x_u, c_d, c_u, w_d, w_u, gain, cand, outer, inner, g_d, g_u, loss, cot):
    is_first = meta[1] == 0
    is_last = meta[1] == meta[2] - 1
    is_even = lax.rem(meta[1], 2) == 0

    def fill(ahead, behind):
        act = tokens_of(received, 0)
        work = (
            (1, x_u, c_u, w_u, behind.at[0], ahead.at[1], g_u, is_first),
            (0, x_d, c_d, w_d, ahead.at[0], behind.at[1], g_d, is_last),
        )
        for side, x, c, w, y, dx, g, end in work:
            wide = x[...].astype(F32)
            y[...] = (wide + nn(act, at_rows(w[R : 2 * R], side))).astype(BF16)
            cot[...] = c[...].astype(F32)

            @pl.when(end)
            def _():
                high, low = halves(columns_of(gain, cand))
                grad = tokens_of(received, PER)
                final = x[...].astype(F32) + nn(act, at_rows(w[R : 2 * R], side))
                cot[...] = nn(grad, high) + nn(grad, low) - coefficient(received, 4) * final

            held = cot[...]
            back = held + nn(act, at_rows(w[0:R], 2 + side)) - coefficient(received, 2 * side) * wide
            dx[...] = back.astype(BF16)
            by_cot = tn(act, held.astype(BF16))
            by_x = tn(act, x[...])
            grads = jnp.concatenate(
                [by_x[64 + R * side : 64 + R * side + R], by_cot[R * side : R * side + R]], axis=0
            )
            g[...] = grads.astype(g.dtype)

    @pl.when(is_even)
    def _():
        fill(inner, outer)

    @pl.when(jnp.logical_not(is_even))
    def _():
        fill(outer, inner)

    rows = jnp.sum(received[:, CROSS:BACK_ROWS, :].astype(F32), axis=0)
    total = rows[6:7] + rows[7:8] + rows[8:9]
    loss[...] = jnp.broadcast_to(total, loss.shape)


def finish(
    meta, outer, inner, g_d, mate, losses, down_next, up_next, down_back, up_back, grad_a, grad_b, loss, sems
):
    is_even = lax.rem(meta[1], 2) == 0

    def copies_of(ahead, behind):
        return [
            pltpu.make_async_copy(ahead.at[0], down_next, sems.at[0]),
            pltpu.make_async_copy(behind.at[0], up_next, sems.at[1]),
            pltpu.make_async_copy(behind.at[1], down_back, sems.at[2]),
            pltpu.make_async_copy(ahead.at[1], up_back, sems.at[3]),
        ]

    @pl.when(is_even)
    def _():
        for copy in copies_of(outer, inner):
            copy.start()

    @pl.when(jnp.logical_not(is_even))
    def _():
        for copy in copies_of(inner, outer):
            copy.start()

    total = g_d[...] + mate[...].astype(F32)
    grad_a[...] = total[0:R]
    grad_b[...] = total[R : 2 * R]
    loss[0] = jnp.sum(losses[:, 0:1])

    @pl.when(is_even)
    def _():
        for copy in copies_of(outer, inner):
            copy.wait()

    @pl.when(jnp.logical_not(is_even))
    def _():
        for copy in copies_of(inner, outer):
            copy.wait()


def shards(
    down_in,
    up_in,
    down_cot,
    up_cot,
    adapt_a,
    adapt_b,
    head_gain,
    cand,
    down_ids,
    up_ids,
    offsets,
    loss_weights,
):
    sections = lax.axis_size("section")
    groups = lax.axis_size("dp")
    position = lax.axis_index("section")
    place = lax.axis_index("dp")
    tokens, local_width = down_in.shape[1:]
    heads, candidates = head_gain.shape[0], cand.shape[0]
    mirror = [(i, sections - 1 - i) for i in range(sections)]
    inside = [(i, i ^ 1) for i in range(sections)]
    between = [(i, i + 1 if i % 2 else i - 1) for i in range(1, sections - 1)]
    smem = pl.BlockSpec(memory_space=pltpu.SMEM)
    vmem = pl.BlockSpec(memory_space=pltpu.VMEM)
    hbm = pl.BlockSpec(memory_space=pltpu.HBM)
    params = pltpu.CompilerParams(vmem_limit_bytes=48 << 20)
    shape = jax.ShapeDtypeStruct
    wide = shape((tokens, local_width), BF16)
    both = shape((2, tokens, local_width), BF16)

    w_d = pl.pallas_call(
        packed,
        out_shape=shape((2 * R, local_width), BF16),
        in_specs=[hbm] * 2,
        out_specs=vmem,
        scratch_shapes=[pltpu.SemaphoreType.DMA((2,))],
        compiler_params=params,
    )(in_hbm(adapt_a[0].T), in_hbm(adapt_b[0]))
    w_u = lax.ppermute(w_d, "section", mirror)
    sizes = jnp.int32(sections), jnp.int32(head_gain.shape[1])
    meta = jnp.stack([place.astype(jnp.int32), position.astype(jnp.int32), *sizes])
    id_rows = (tokens // LANES, LANES)
    ids = down_ids.reshape(id_rows), up_ids.reshape(id_rows)
    fetched = (down_in[0], up_in[0], down_cot[0], up_cot[0], head_gain, cand, *ids, offsets, loss_weights)

    near = tokens // PER
    rings = [list(range(first, first + near)) for first in range(0, groups, near)]
    partners = [list(members) for members in zip(*rings)]
    send = shape((near, ROWS, LANES), BF16)
    partial, x_d, x_u, c_d, c_u, gain_part, cand_part, ids_d, ids_u, shifts, shares = pl.pallas_call(
        first_partial,
        out_shape=(
            send,
            wide,
            wide,
            wide,
            wide,
            shape((heads, local_width), F32),
            shape((candidates, local_width), BF16),
            shape(id_rows, jnp.int32),
            shape(id_rows, jnp.int32),
            shape(offsets.shape, jnp.int32),
            shape(loss_weights.shape, jnp.int32),
        ),
        in_specs=[smem] + [hbm] * 10 + [vmem],
        out_specs=(vmem,) * 9 + (smem,) * 2,
        scratch_shapes=[pltpu.SemaphoreType.DMA((10,))],
        compiler_params=params,
    )(meta, *(in_hbm(held) for held in fetched), w_d)
    partial = pl.pallas_call(
        second_partial,
        out_shape=send,
        in_specs=[smem] + [vmem] * 7,
        out_specs=vmem,
        compiler_params=params,
    )(meta, partial, x_u, c_u, w_u, w_d, gain_part, cand_part)
    received = lax.all_to_all(partial, "dp", 0, 0, axis_index_groups=rings)
    summed = pl.pallas_call(
        gathered_sum,
        out_shape=shape((ROWS, LANES), BF16),
        in_specs=[vmem],
        out_specs=vmem,
        compiler_params=params,
    )(received)
    received = lax.all_gather(summed, "dp", axis_index_groups=partners)

    back = pl.pallas_call(
        middle,
        out_shape=shape((near, BACK_ROWS, LANES), BF16),
        in_specs=[smem] * 3 + [vmem] * 3,
        out_specs=vmem,
        compiler_params=params,
    )(meta, shifts, shares, received, ids_d, ids_u)
    gathered = lax.all_to_all(back, "dp", 0, 0, axis_index_groups=rings)

    outer, inner, g_d, g_u, loss_rows = pl.pallas_call(
        backward,
        out_shape=(
            both,
            both,
            shape((2 * R, local_width), F32),
            shape((2 * R, local_width), BF16),
            shape((sections, LANES), F32),
        ),
        in_specs=[smem] + [vmem] * 9,
        out_specs=(vmem,) * 5,
        scratch_shapes=[pltpu.VMEM((tokens, local_width), F32)],
        compiler_params=params,
    )(meta, gathered, x_d, x_u, c_d, c_u, w_d, w_u, gain_part, cand_part)
    outer = lax.ppermute(outer, "section", between)
    inner = lax.ppermute(inner, "section", inside)
    mate = lax.ppermute(g_u, "section", mirror)
    losses = lax.all_to_all(loss_rows, "section", 0, 0, tiled=True)
    down_next, up_next, down_back, up_back, grad_a, grad_b, loss = pl.pallas_call(
        finish,
        out_shape=(
            wide,
            wide,
            wide,
            wide,
            shape((R, local_width), F32),
            shape((R, local_width), F32),
            shape((1,), F32),
        ),
        in_specs=[smem] + [vmem] * 5,
        out_specs=(hbm,) * 4 + (vmem, vmem, smem),
        scratch_shapes=[pltpu.SemaphoreType.DMA((4,))],
        compiler_params=params,
    )(meta, outer, inner, g_d, mate, losses)
    return (
        down_next[None],
        up_next[None],
        down_back[None],
        up_back[None],
        grad_a.T[None],
        grad_b[None],
        loss,
    )


def solution(mesh):
    in_specs = (
        P("section", None, "dp"),
        P("section", None, "dp"),
        P("section", None, "dp"),
        P("section", None, "dp"),
        P("section", "dp", None),
        P("section", None, "dp"),
        P(),
        P(),
        P(),
        P(),
        P(),
        P(),
    )
    out_specs = (
        P("section", None, "dp"),
        P("section", None, "dp"),
        P("section", None, "dp"),
        P("section", None, "dp"),
        P("section", "dp", None),
        P("section", None, "dp"),
        P(),
    )
    return jax.shard_map(shards, mesh=mesh, in_specs=in_specs, out_specs=out_specs, check_vma=False)
```

```python
import jax
import jax.numpy as jnp
from jax import lax
from jax.experimental import pallas as pl
from jax.experimental.pallas import tpu as pltpu
from jax.sharding import PartitionSpec as P

EPS = 1e-05
F32 = jnp.float32
BF16 = jnp.bfloat16
HIGH = lax.Precision.HIGHEST
R = 32
M = 32
LANES = 128
PER = 64
PLAIN = PER + 16
CROSS = PLAIN + PER
ROWS = CROSS + R
BACK_ROWS = PLAIN + PER


def nt(a, b, precision=None):
    return lax.dot_general(a, b, (((1,), (1,)), ((), ())), precision=precision, preferred_element_type=F32)


def nn(a, b, precision=None):
    return lax.dot_general(a, b, (((1,), (0,)), ((), ())), precision=precision, preferred_element_type=F32)


def tn(a, b):
    return lax.dot_general(a, b, (((0,), (0,)), ((), ())), preferred_element_type=F32)


def halves(value):
    high = value.astype(BF16)
    return high, (value - high.astype(F32)).astype(BF16)


def columns_of(gain_ref, cand_ref):
    cand = cand_ref[...].astype(F32)
    return jnp.concatenate([gain_ref[k : k + 1, :] * cand for k in range(gain_ref.shape[0])], axis=0)


def squares_row(block):
    wide = block.astype(F32)
    ones = jnp.ones((8, wide.shape[1]), BF16)
    high, low = halves(wide * wide)
    return (nt(ones, high) + nt(ones, low))[0:1, :]


def gated(weights, flag):
    return jnp.where(flag, weights.astype(F32), 0.0).astype(BF16)


def in_hbm(value):
    return pltpu.with_memory_space_constraint(value, pltpu.HBM)


def packed(a_hbm, b_hbm, w, sems):
    copies = [
        pltpu.make_async_copy(a_hbm, w.at[0:R], sems.at[0]),
        pltpu.make_async_copy(b_hbm, w.at[R : 2 * R], sems.at[1]),
    ]
    for copy in copies:
        copy.start()
    for copy in copies:
        copy.wait()


def first_partial(
    meta,
    x_d_hbm,
    x_u_hbm,
    c_d_hbm,
    c_u_hbm,
    gain_hbm,
    cand_hbm,
    ids_d_hbm,
    ids_u_hbm,
    offsets_hbm,
    weights_hbm,
    w_d,
    out,
    x_d,
    x_u,
    c_d,
    c_u,
    gain,
    cand,
    ids_d,
    ids_u,
    offsets,
    weights,
    sems,
):
    sections = meta[2]
    is_first = meta[1] == 0
    is_last = meta[1] == sections - 1
    chunks = out.shape[0]
    width = x_d.shape[1]
    here = pl.ds(pl.multiple_of(meta[0] * width, width), width)
    get_x_d = pltpu.make_async_copy(x_d_hbm, x_d, sems.at[0])
    get_c_d = pltpu.make_async_copy(c_d_hbm, c_d, sems.at[1])
    get_x_u = pltpu.make_async_copy(x_u_hbm, x_u, sems.at[2])
    get_c_u = pltpu.make_async_copy(c_u_hbm, c_u, sems.at[3])
    get_gain = pltpu.make_async_copy(gain_hbm.at[:, here], gain, sems.at[4])
    get_cand = pltpu.make_async_copy(cand_hbm.at[:, here], cand, sems.at[5])
    get_ids_d = pltpu.make_async_copy(ids_d_hbm, ids_d, sems.at[6])
    get_ids_u = pltpu.make_async_copy(ids_u_hbm, ids_u, sems.at[7])
    get_offsets = pltpu.make_async_copy(offsets_hbm, offsets, sems.at[8])
    get_weights = pltpu.make_async_copy(weights_hbm, weights, sems.at[9])
    small = (get_ids_d, get_ids_u, get_offsets, get_weights)
    for copy in (get_x_d, get_c_d, get_x_u, get_gain, get_cand, get_c_u, *small):
        copy.start()
    a_d, b_d = w_d[0:R], w_d[R : 2 * R]
    zero = jnp.zeros((R, width), BF16)
    wx = jnp.concatenate([a_d, zero, gated(b_d, is_last), zero], axis=0)
    wc = jnp.concatenate([zero, zero, gated(b_d, jnp.logical_not(is_last)), zero], axis=0)
    out[:, CROSS:ROWS, :] = jnp.zeros((chunks, R, LANES), BF16)
    get_x_d.wait()
    get_c_d.wait()
    main = nt(x_d[...], wx) + nt(c_d[...], wc)
    out[:, 0:PER, :] = main.astype(BF16).reshape(chunks, PER, LANES)
    get_x_u.wait()
    rows = []
    for block in (x_d[...], x_u[...]):
        row = squares_row(block)
        high = row.astype(BF16).astype(F32)
        rows += [high, row - high]
    per = LANES // PER
    pad = jnp.zeros((8, LANES), F32)
    for j in range(chunks):
        start = (j // per) * LANES
        piece = [row[:, start : start + LANES] for row in rows]
        tail = jnp.concatenate([pad] + piece + [pad[0:4]], axis=0)
        out[j, PER:PLAIN, :] = tail.astype(BF16)
    get_gain.wait()
    get_cand.wait()

    def logits_of(block):
        high, low = halves(columns_of(gain, cand))
        value = nt(block, high) + nt(block, low)
        out[:, PLAIN:CROSS, :] = value.astype(BF16).reshape(chunks, PER, LANES)

    @pl.when(is_last)
    def _():
        logits_of(x_d[...])

    @pl.when(is_first)
    def _():
        logits_of(x_u[...])

    @pl.when(jnp.logical_not(jnp.logical_or(is_first, is_last)))
    def _():
        out[:, PLAIN:CROSS, :] = jnp.zeros((chunks, PER, LANES), BF16)

    get_c_u.wait()
    for copy in small:
        copy.wait()


def second_partial(meta, partial, x_u, c_u, w_u, w_d, gain, cand, out):
    is_first = meta[1] == 0
    is_last = meta[1] == meta[2] - 1
    chunks = out.shape[0]
    width = x_u.shape[1]
    a_u, b_u = w_u[0:R], w_u[R : 2 * R]
    zero = jnp.zeros((R, width), BF16)
    wx = jnp.concatenate([zero, a_u, zero, gated(b_u, is_first)], axis=0)
    wc = jnp.concatenate([zero, zero, zero, gated(b_u, jnp.logical_not(is_first))], axis=0)
    main = nt(x_u[...], wx) + nt(c_u[...], wc)
    main = main.reshape(chunks, PER, LANES) + partial[:, 0:PER, :].astype(F32)
    out[:, 0:PER, :] = main.astype(BF16)
    rows = out.shape[1]
    out[:, PER:rows, :] = partial[:, PER:rows, :]
    if rows > PLAIN:
        b_d = w_d[R : 2 * R]
        b_e = jnp.where(is_last, b_d.astype(F32), b_u.astype(F32)).astype(BF16)
        high, low = halves(columns_of(gain, cand))
        cross = nt(b_e, high) + nt(b_e, low)
        own = nt(b_e, b_e)
        folded = jnp.concatenate([own[8 * r : 8 * r + 8] for r in range(4)], axis=1)
        tail = jnp.concatenate([folded, jnp.zeros((8, LANES), F32)], axis=0)
        out[:, CROSS:ROWS, :] = jnp.broadcast_to(cross.astype(BF16)[None], (chunks, R, LANES))
        held = partial[:, PER:PLAIN, :].astype(F32) + tail[None]
        out[:, PER:PLAIN, :] = held.astype(BF16)


def gathered_sum(received, out):
    total = jnp.sum(received[...].astype(F32), axis=0)
    folded = total[PER : PER + 8]
    rows = [folded]
    for side in range(2):
        first = PER + 8 + 2 * side
        row = total[first : first + 1] + total[first + 1 : first + 2]
        high = row.astype(BF16).astype(F32)
        rows += [high, row - high]
    rows += [jnp.zeros((4, LANES), F32)]
    out[0:PER] = total[0:PER].astype(BF16)
    out[PER:PLAIN] = jnp.concatenate(rows, axis=0).astype(BF16)
    if total.shape[0] > PLAIN:
        out[PLAIN:] = total[PLAIN:].astype(BF16)


def middle(meta, offsets, loss_weights, received, down_ids, up_ids, out):
    chunks = out.shape[0]
    place = lax.rem(meta[0], chunks)
    is_first = meta[1] == 0
    is_last = meta[1] == meta[2] - 1
    ends = out.shape[1] > PLAIN
    inverse = 1.0 / meta[3].astype(F32)
    heads = LANES // R
    total = received[0].astype(F32) + received[1].astype(F32)
    main, folded, square_rows = total[0:PER], total[PER : PER + 8], total[PER + 8 : PER + 12]
    lane = lax.broadcasted_iota(jnp.int32, (PER, LANES), 1)
    token = lax.broadcasted_iota(jnp.int32, (PER, LANES), 0)
    spot = lax.rem(token, M)
    sequences = chunks * (PER // M)
    base = PER * lax.rem(place, LANES // PER)

    def column(row):
        return jnp.sum(jnp.where(lane == base + token, row, 0.0), axis=1, keepdims=True)

    square_d = column(square_rows[0:1] + square_rows[1:2])
    square_u = column(square_rows[2:3] + square_rows[3:4])
    scale_d = lax.rsqrt(square_d * inverse + EPS)
    scale_u = lax.rsqrt(square_u * inverse + EPS)
    down_lane = lane < R
    up_lane = jnp.logical_and(lane >= R, lane < 2 * R)
    low_lane = lane < 2 * R
    scale = jnp.where(down_lane, scale_d, scale_u)
    projected = jnp.where(low_lane, main, 0.0)
    pre = projected * scale
    sigma = jax.nn.sigmoid(pre)
    act = pre * sigma

    dg = pltpu.roll(main, 2 * R, axis=1)
    columns = []
    if ends:
        act_e = jnp.where(is_first, act[:, R : 2 * R], act[:, 0:R])
        cot_e = jnp.where(is_first, main[:, 3 * R :], main[:, 2 * R : 3 * R])
        own = jnp.concatenate([folded[:, R * r : R * r + R] for r in range(4)], axis=0)
        act_own = nn(act_e, own, HIGH)
        out_b = cot_e + act_own
        square_e = jnp.where(is_first, square_u, square_d)
        square_e = square_e + jnp.sum(act_e * (cot_e + out_b), axis=1, keepdims=True)
        scale_e = lax.rsqrt(jnp.maximum(square_e, 0.0) * inverse + EPS)
        cross = total[CROSS:ROWS]
        raw = total[PLAIN:CROSS] + nn(act_e, cross, HIGH)
        logits = raw * scale_e
        block = lax.div(place, LANES // PER)
        ids_d = down_ids[pl.ds(block, 1), :]
        ids_u = up_ids[pl.ds(block, 1), :]
        ids = jnp.where(is_first, ids_u, ids_d).astype(F32)
        group = lax.div(lane, R)
        within = lax.rem(lane, R)
        weight_sum = jnp.float32(0.0)
        for k in range(heads):
            weight_sum = weight_sum + loss_weights[k].astype(F32)
        top = jnp.zeros((PER, LANES), F32)
        target = jnp.zeros((PER, LANES), F32)
        weight = jnp.zeros((PER, LANES), F32)
        for k in range(heads):
            mine = group == k
            shift = offsets[k]
            largest = jnp.max(jnp.where(mine, logits, -jnp.inf), axis=1, keepdims=True)
            wanted = jnp.sum(jnp.where(lane == base + token + shift, ids, 0.0), axis=1, keepdims=True)
            factor = loss_weights[k].astype(F32) / weight_sum / ((M - shift) * sequences).astype(F32)
            valid = jnp.where(spot + shift < M, factor, 0.0)
            top = jnp.where(mine, largest, top)
            target = jnp.where(mine, wanted, target)
            weight = jnp.where(mine, valid, weight)
        power = jnp.exp(logits - top)
        below = jnp.ones((PER, LANES), F32)
        for k in range(heads):
            mine = group == k
            below = jnp.where(mine, jnp.sum(jnp.where(mine, power, 0.0), axis=1, keepdims=True), below)
        hit = jnp.where(within == target.astype(jnp.int32), 1.0, 0.0)
        per_lane = hit * (top + jnp.log(below) - logits) * weight
        loss = jnp.sum(jnp.sum(per_lane, axis=1, keepdims=True), axis=0, keepdims=True)
        grad = weight * (power / below - hit)
        grad_cols = grad * scale_e
        coef_e = jnp.sum(grad * raw, axis=1, keepdims=True) * scale_e * scale_e * scale_e * inverse
        dg_e = nt(grad_cols, cross, HIGH) - coef_e * out_b
        dg_wide = jnp.concatenate([dg_e] * 4, axis=1)
        replace = jnp.logical_or(jnp.logical_and(is_last, down_lane), jnp.logical_and(is_first, up_lane))
        dg = jnp.where(replace, dg_wide, dg)
        columns = [coef_e]
    d_pre = jnp.where(low_lane, dg * sigma * (1.0 + pre * (1.0 - sigma)), 0.0)
    d_scaled = d_pre * scale
    moved = d_pre * projected
    coef_d = jnp.sum(jnp.where(down_lane, moved, 0.0), axis=1, keepdims=True)
    coef_u = jnp.sum(jnp.where(up_lane, moved, 0.0), axis=1, keepdims=True)
    coef_d = coef_d * scale_d * scale_d * scale_d * inverse
    coef_u = coef_u * scale_u * scale_u * scale_u * inverse
    both = jnp.where(low_lane, act, pltpu.roll(d_scaled, 2 * R, axis=1))

    def parts_of(row):
        high = row.astype(BF16).astype(F32)
        low = (row - high).astype(BF16).astype(F32)
        return [high, low, row - high - low]

    rows = []
    for col in (coef_d, coef_u, *columns):
        row = jnp.sum(jnp.where(lane == token, col, 0.0), axis=0, keepdims=True)
        rows += parts_of(row)[0:2]
    if ends:
        rows += parts_of(jnp.broadcast_to(loss, (1, LANES)))
    rows += [jnp.zeros((16 - len(rows), LANES), F32)]
    chunk = jnp.concatenate([both] + rows + ([grad_cols] if ends else []), axis=0)
    out[...] = jnp.broadcast_to(chunk.astype(BF16)[None], out.shape)


def tokens_of(received, first):
    chunks = received.shape[0]
    return received[:, first : first + PER, :].reshape(chunks * PER, LANES)


def coefficient(received, row):
    chunks = received.shape[0]
    lane = lax.broadcasted_iota(jnp.int32, (PER, LANES), 1)
    token = lax.broadcasted_iota(jnp.int32, (PER, LANES), 0)
    cols = []
    for j in range(chunks):
        rows = received[j, PER:PLAIN, :].astype(F32)
        both = rows[row : row + 1] + rows[row + 1 : row + 2]
        cols.append(jnp.sum(jnp.where(lane == token, both, 0.0), axis=1, keepdims=True))
    return jnp.concatenate(cols, axis=0)


def at_rows(weights, group):
    zero = jnp.zeros_like(weights)
    return jnp.concatenate([weights if k == group else zero for k in range(LANES // R)], axis=0)


def backward(meta, received, x_d, x_u, c_d, c_u, w_d, w_u, gain, cand, outer, inner, g_d, g_u, loss, cot):
    is_first = meta[1] == 0
    is_last = meta[1] == meta[2] - 1
    is_even = lax.rem(meta[1], 2) == 0

    def fill(ahead, behind):
        act = tokens_of(received, 0)
        work = (
            (1, x_u, c_u, w_u, behind.at[0], ahead.at[1], g_u, is_first),
            (0, x_d, c_d, w_d, ahead.at[0], behind.at[1], g_d, is_last),
        )
        for side, x, c, w, y, dx, g, end in work:
            wide = x[...].astype(F32)
            y[...] = (wide + nn(act, at_rows(w[R : 2 * R], side))).astype(BF16)
            cot[...] = c[...].astype(F32)

            if received.shape[1] > PLAIN:

                @pl.when(end)
                def _():
                    high, low = halves(columns_of(gain, cand))
                    grad = tokens_of(received, PLAIN)
                    final = x[...].astype(F32) + nn(act, at_rows(w[R : 2 * R], side))
                    cot[...] = nn(grad, high) + nn(grad, low) - coefficient(received, 4) * final

            held = cot[...]
            back = held + nn(act, at_rows(w[0:R], 2 + side)) - coefficient(received, 2 * side) * wide
            dx[...] = back.astype(BF16)
            by_cot = tn(act, held.astype(BF16))
            by_x = tn(act, x[...])
            grads = jnp.concatenate(
                [by_x[64 + R * side : 64 + R * side + R], by_cot[R * side : R * side + R]], axis=0
            )
            g[...] = grads.astype(g.dtype)

    @pl.when(is_even)
    def _():
        fill(inner, outer)

    @pl.when(jnp.logical_not(is_even))
    def _():
        fill(outer, inner)

    total = jnp.zeros((1, LANES), F32)
    if received.shape[1] > PLAIN:
        rows = jnp.sum(received[:, PER:PLAIN, :].astype(F32), axis=0)
        total = rows[6:7] + rows[7:8] + rows[8:9]
    loss[...] = jnp.broadcast_to(total, loss.shape)


def finish(
    meta, outer, inner, g_d, mate, losses, down_next, up_next, down_back, up_back, grad_a, grad_b, loss, sems
):
    is_even = lax.rem(meta[1], 2) == 0

    def copies_of(ahead, behind):
        return [
            pltpu.make_async_copy(ahead.at[0], down_next, sems.at[0]),
            pltpu.make_async_copy(behind.at[0], up_next, sems.at[1]),
            pltpu.make_async_copy(behind.at[1], down_back, sems.at[2]),
            pltpu.make_async_copy(ahead.at[1], up_back, sems.at[3]),
        ]

    @pl.when(is_even)
    def _():
        for copy in copies_of(outer, inner):
            copy.start()

    @pl.when(jnp.logical_not(is_even))
    def _():
        for copy in copies_of(inner, outer):
            copy.start()

    total = g_d[...] + mate[...].astype(F32)
    grad_a[...] = total[0:R]
    grad_b[...] = total[R : 2 * R]
    loss[0] = jnp.sum(losses[:, 0:1])

    @pl.when(is_even)
    def _():
        for copy in copies_of(outer, inner):
            copy.wait()

    @pl.when(jnp.logical_not(is_even))
    def _():
        for copy in copies_of(inner, outer):
            copy.wait()


def shards(
    down_in,
    up_in,
    down_cot,
    up_cot,
    adapt_a,
    adapt_b,
    head_gain,
    cand,
    down_ids,
    up_ids,
    offsets,
    loss_weights,
):
    sections = lax.axis_size("section")
    groups = lax.axis_size("dp")
    position = lax.axis_index("section")
    place = lax.axis_index("dp")
    tokens, local_width = down_in.shape[1:]
    heads, candidates = head_gain.shape[0], cand.shape[0]
    mirror = [(i, sections - 1 - i) for i in range(sections)]
    inside = [(i, i ^ 1) for i in range(sections)]
    between = [(i, i + 1 if i % 2 else i - 1) for i in range(1, sections - 1)]
    smem = pl.BlockSpec(memory_space=pltpu.SMEM)
    vmem = pl.BlockSpec(memory_space=pltpu.VMEM)
    hbm = pl.BlockSpec(memory_space=pltpu.HBM)
    params = pltpu.CompilerParams(vmem_limit_bytes=48 << 20)
    shape = jax.ShapeDtypeStruct
    wide = shape((tokens, local_width), BF16)
    both = shape((2, tokens, local_width), BF16)

    w_d = pl.pallas_call(
        packed,
        out_shape=shape((2 * R, local_width), BF16),
        in_specs=[hbm] * 2,
        out_specs=vmem,
        scratch_shapes=[pltpu.SemaphoreType.DMA((2,))],
        compiler_params=params,
    )(in_hbm(adapt_a[0].T), in_hbm(adapt_b[0]))
    w_u = lax.ppermute(w_d, "section", mirror)
    sizes = jnp.int32(sections), jnp.int32(head_gain.shape[1])
    meta = jnp.stack([place.astype(jnp.int32), position.astype(jnp.int32), *sizes])
    id_rows = (tokens // LANES, LANES)
    ids = down_ids.reshape(id_rows), up_ids.reshape(id_rows)
    fetched = (down_in[0], up_in[0], down_cot[0], up_cot[0], head_gain, cand, *ids, offsets, loss_weights)

    near = tokens // PER
    rings = [list(range(first, first + near)) for first in range(0, groups, near)]
    partners = [list(members) for members in zip(*rings)]
    send = shape((near, ROWS, LANES), BF16)
    partial, x_d, x_u, c_d, c_u, gain_part, cand_part, ids_d, ids_u, shifts, shares = pl.pallas_call(
        first_partial,
        out_shape=(
            send,
            wide,
            wide,
            wide,
            wide,
            shape((heads, local_width), F32),
            shape((candidates, local_width), BF16),
            shape(id_rows, jnp.int32),
            shape(id_rows, jnp.int32),
            shape(offsets.shape, jnp.int32),
            shape(loss_weights.shape, jnp.int32),
        ),
        in_specs=[smem] + [hbm] * 10 + [vmem],
        out_specs=(vmem,) * 9 + (smem,) * 2,
        scratch_shapes=[pltpu.SemaphoreType.DMA((10,))],
        compiler_params=params,
    )(meta, *(in_hbm(held) for held in fetched), w_d)

    def over_dp(rows, back_rows):
        def run(meta, partial, x_d, x_u, c_d, c_u, w_d, w_u, gain_part, cand_part, shifts, shares, ids_d, ids_u):
            chunk = pl.pallas_call(
                second_partial,
                out_shape=shape((near, rows, LANES), BF16),
                in_specs=[smem] + [vmem] * 7,
                out_specs=vmem,
                compiler_params=params,
            )(meta, partial, x_u, c_u, w_u, w_d, gain_part, cand_part)
            received = lax.all_to_all(chunk, "dp", 0, 0, axis_index_groups=rings)
            summed = pl.pallas_call(
                gathered_sum,
                out_shape=shape((rows, LANES), BF16),
                in_specs=[vmem],
                out_specs=vmem,
                compiler_params=params,
            )(received)
            received = lax.all_gather(summed, "dp", axis_index_groups=partners)
            back = pl.pallas_call(
                middle,
                out_shape=shape((near, back_rows, LANES), BF16),
                in_specs=[smem] * 3 + [vmem] * 3,
                out_specs=vmem,
                compiler_params=params,
            )(meta, shifts, shares, received, ids_d, ids_u)
            gathered = lax.all_to_all(back, "dp", 0, 0, axis_index_groups=rings)
            return pl.pallas_call(
                backward,
                out_shape=(
                    both,
                    both,
                    shape((2 * R, local_width), F32),
                    shape((2 * R, local_width), BF16),
                    shape((sections, LANES), F32),
                ),
                in_specs=[smem] + [vmem] * 9,
                out_specs=(vmem,) * 5,
                scratch_shapes=[pltpu.VMEM((tokens, local_width), F32)],
                compiler_params=params,
            )(meta, gathered, x_d, x_u, c_d, c_u, w_d, w_u, gain_part, cand_part)

        return run

    held = (meta, partial, x_d, x_u, c_d, c_u, w_d, w_u, gain_part, cand_part, shifts, shares, ids_d, ids_u)
    is_end = jnp.logical_or(position == 0, position == sections - 1)
    outer, inner, g_d, g_u, loss_rows = lax.cond(
        is_end, over_dp(ROWS, BACK_ROWS), over_dp(PLAIN, PLAIN), *held
    )
    outer = lax.ppermute(outer, "section", between)
    inner = lax.ppermute(inner, "section", inside)
    mate = lax.ppermute(g_u, "section", mirror)
    losses = lax.all_to_all(loss_rows, "section", 0, 0, tiled=True)
    down_next, up_next, down_back, up_back, grad_a, grad_b, loss = pl.pallas_call(
        finish,
        out_shape=(
            wide,
            wide,
            wide,
            wide,
            shape((R, local_width), F32),
            shape((R, local_width), F32),
            shape((1,), F32),
        ),
        in_specs=[smem] + [vmem] * 5,
        out_specs=(hbm,) * 4 + (vmem, vmem, smem),
        scratch_shapes=[pltpu.SemaphoreType.DMA((4,))],
        compiler_params=params,
    )(meta, outer, inner, g_d, mate, losses)
    return (
        down_next[None],
        up_next[None],
        down_back[None],
        up_back[None],
        grad_a.T[None],
        grad_b[None],
        loss,
    )


def solution(mesh):
    in_specs = (
        P("section", None, "dp"),
        P("section", None, "dp"),
        P("section", None, "dp"),
        P("section", None, "dp"),
        P("section", "dp", None),
        P("section", None, "dp"),
        P(),
        P(),
        P(),
        P(),
        P(),
        P(),
    )
    out_specs = (
        P("section", None, "dp"),
        P("section", None, "dp"),
        P("section", None, "dp"),
        P("section", None, "dp"),
        P("section", "dp", None),
        P("section", None, "dp"),
        P(),
    )
    return jax.shard_map(shards, mesh=mesh, in_specs=in_specs, out_specs=out_specs, check_vma=False)
```

```python
import jax
import jax.numpy as jnp
from jax import lax
from jax.experimental import pallas as pl
from jax.experimental.pallas import tpu as pltpu
from jax.sharding import PartitionSpec as P

EPS = 1e-05
F32 = jnp.float32
BF16 = jnp.bfloat16
HIGH = lax.Precision.HIGHEST
R = 32
M = 32
LANES = 128
PER = 64
PLAIN = PER + 16
CROSS = PLAIN + PER
ROWS = CROSS + R
BACK_ROWS = PLAIN + PER


def nt(a, b, precision=None):
    return lax.dot_general(a, b, (((1,), (1,)), ((), ())), precision=precision, preferred_element_type=F32)


def nn(a, b, precision=None):
    return lax.dot_general(a, b, (((1,), (0,)), ((), ())), precision=precision, preferred_element_type=F32)


def tn(a, b):
    return lax.dot_general(a, b, (((0,), (0,)), ((), ())), preferred_element_type=F32)


def halves(value):
    high = value.astype(BF16)
    return high, (value - high.astype(F32)).astype(BF16)


def columns_of(gain_ref, cand_ref):
    cand = cand_ref[...].astype(F32)
    return jnp.concatenate([gain_ref[k : k + 1, :] * cand for k in range(gain_ref.shape[0])], axis=0)


def squares_row(block):
    wide = block.astype(F32)
    ones = jnp.ones((8, wide.shape[1]), BF16)
    high, low = halves(wide * wide)
    return (nt(ones, high) + nt(ones, low))[0:1, :]


def gated(weights, flag):
    return jnp.where(flag, weights.astype(F32), 0.0).astype(BF16)


def in_hbm(value):
    return pltpu.with_memory_space_constraint(value, pltpu.HBM)


def packed(a_hbm, b_hbm, w, sems):
    copies = [
        pltpu.make_async_copy(a_hbm, w.at[0:R], sems.at[0]),
        pltpu.make_async_copy(b_hbm, w.at[R : 2 * R], sems.at[1]),
    ]
    for copy in copies:
        copy.start()
    for copy in copies:
        copy.wait()


def first_partial(
    meta,
    x_d_hbm,
    x_u_hbm,
    c_d_hbm,
    c_u_hbm,
    gain_hbm,
    cand_hbm,
    ids_d_hbm,
    ids_u_hbm,
    offsets_hbm,
    weights_hbm,
    w_d,
    out,
    x_d,
    x_u,
    c_d,
    c_u,
    gain,
    cand,
    ids_d,
    ids_u,
    offsets,
    weights,
    sems,
):
    sections = meta[2]
    is_first = meta[1] == 0
    is_last = meta[1] == sections - 1
    chunks = out.shape[0]
    width = x_d.shape[1]
    here = pl.ds(pl.multiple_of(meta[0] * width, width), width)
    get_x_d = pltpu.make_async_copy(x_d_hbm, x_d, sems.at[0])
    get_c_d = pltpu.make_async_copy(c_d_hbm, c_d, sems.at[1])
    get_x_u = pltpu.make_async_copy(x_u_hbm, x_u, sems.at[2])
    get_c_u = pltpu.make_async_copy(c_u_hbm, c_u, sems.at[3])
    get_gain = pltpu.make_async_copy(gain_hbm.at[:, here], gain, sems.at[4])
    get_cand = pltpu.make_async_copy(cand_hbm.at[:, here], cand, sems.at[5])
    get_ids_d = pltpu.make_async_copy(ids_d_hbm, ids_d, sems.at[6])
    get_ids_u = pltpu.make_async_copy(ids_u_hbm, ids_u, sems.at[7])
    get_offsets = pltpu.make_async_copy(offsets_hbm, offsets, sems.at[8])
    get_weights = pltpu.make_async_copy(weights_hbm, weights, sems.at[9])
    small = (get_ids_d, get_ids_u, get_offsets, get_weights)
    for copy in (get_x_d, get_c_d, get_x_u, get_gain, get_cand, get_c_u, *small):
        copy.start()
    a_d, b_d = w_d[0:R], w_d[R : 2 * R]
    zero = jnp.zeros((R, width), BF16)
    wx = jnp.concatenate([a_d, zero, gated(b_d, is_last), zero], axis=0)
    wc = jnp.concatenate([zero, zero, gated(b_d, jnp.logical_not(is_last)), zero], axis=0)
    out[:, CROSS:ROWS, :] = jnp.zeros((chunks, R, LANES), BF16)
    get_x_d.wait()
    get_c_d.wait()
    main = nt(x_d[...], wx) + nt(c_d[...], wc)
    out[:, 0:PER, :] = main.astype(BF16).reshape(chunks, PER, LANES)
    get_x_u.wait()
    rows = []
    for block in (x_d[...], x_u[...]):
        row = squares_row(block)
        high = row.astype(BF16).astype(F32)
        rows += [high, row - high]
    per = LANES // PER
    pad = jnp.zeros((8, LANES), F32)
    for j in range(chunks):
        start = (j // per) * LANES
        piece = [row[:, start : start + LANES] for row in rows]
        tail = jnp.concatenate([pad] + piece + [pad[0:4]], axis=0)
        out[j, PER:PLAIN, :] = tail.astype(BF16)
    get_gain.wait()
    get_cand.wait()

    def logits_of(block):
        high, low = halves(columns_of(gain, cand))
        value = nt(block, high) + nt(block, low)
        out[:, PLAIN:CROSS, :] = value.astype(BF16).reshape(chunks, PER, LANES)

    @pl.when(is_last)
    def _():
        logits_of(x_d[...])

    @pl.when(is_first)
    def _():
        logits_of(x_u[...])

    @pl.when(jnp.logical_not(jnp.logical_or(is_first, is_last)))
    def _():
        out[:, PLAIN:CROSS, :] = jnp.zeros((chunks, PER, LANES), BF16)

    get_c_u.wait()
    for copy in small:
        copy.wait()


def second_partial(meta, partial, x_u, c_u, w_u, w_d, gain, cand, out):
    is_first = meta[1] == 0
    is_last = meta[1] == meta[2] - 1
    chunks = out.shape[0]
    width = x_u.shape[1]
    a_u, b_u = w_u[0:R], w_u[R : 2 * R]
    zero = jnp.zeros((R, width), BF16)
    wx = jnp.concatenate([zero, a_u, zero, gated(b_u, is_first)], axis=0)
    wc = jnp.concatenate([zero, zero, zero, gated(b_u, jnp.logical_not(is_first))], axis=0)
    main = nt(x_u[...], wx) + nt(c_u[...], wc)
    main = main.reshape(chunks, PER, LANES) + partial[:, 0:PER, :].astype(F32)
    out[:, 0:PER, :] = main.astype(BF16)
    rows = out.shape[1]
    out[:, PER:rows, :] = partial[:, PER:rows, :]
    if rows > PLAIN:
        b_d = w_d[R : 2 * R]
        b_e = jnp.where(is_last, b_d.astype(F32), b_u.astype(F32)).astype(BF16)
        high, low = halves(columns_of(gain, cand))
        cross = nt(b_e, high) + nt(b_e, low)
        own = nt(b_e, b_e)
        folded = jnp.concatenate([own[8 * r : 8 * r + 8] for r in range(4)], axis=1)
        tail = jnp.concatenate([folded, jnp.zeros((8, LANES), F32)], axis=0)
        out[:, CROSS:ROWS, :] = jnp.broadcast_to(cross.astype(BF16)[None], (chunks, R, LANES))
        held = partial[:, PER:PLAIN, :].astype(F32) + tail[None]
        out[:, PER:PLAIN, :] = held.astype(BF16)


def gathered_sum(received, out):
    total = jnp.sum(received[...].astype(F32), axis=0)
    folded = total[PER : PER + 8]
    rows = [folded]
    for side in range(2):
        first = PER + 8 + 2 * side
        row = total[first : first + 1] + total[first + 1 : first + 2]
        high = row.astype(BF16).astype(F32)
        rows += [high, row - high]
    rows += [jnp.zeros((4, LANES), F32)]
    out[0:PER] = total[0:PER].astype(BF16)
    out[PER:PLAIN] = jnp.concatenate(rows, axis=0).astype(BF16)
    if total.shape[0] > PLAIN:
        out[PLAIN:] = total[PLAIN:].astype(BF16)


def middle(meta, offsets, loss_weights, received, down_ids, up_ids, out):
    chunks = out.shape[0]
    place = lax.rem(meta[0], chunks)
    is_first = meta[1] == 0
    is_last = meta[1] == meta[2] - 1
    ends = out.shape[1] > PLAIN
    inverse = 1.0 / meta[3].astype(F32)
    heads = LANES // R
    total = received[0].astype(F32) + received[1].astype(F32)
    main, folded, square_rows = total[0:PER], total[PER : PER + 8], total[PER + 8 : PER + 12]
    lane = lax.broadcasted_iota(jnp.int32, (PER, LANES), 1)
    token = lax.broadcasted_iota(jnp.int32, (PER, LANES), 0)
    spot = lax.rem(token, M)
    sequences = chunks * (PER // M)
    base = PER * lax.rem(place, LANES // PER)

    def column(row):
        return jnp.sum(jnp.where(lane == base + token, row, 0.0), axis=1, keepdims=True)

    square_d = column(square_rows[0:1] + square_rows[1:2])
    square_u = column(square_rows[2:3] + square_rows[3:4])
    scale_d = lax.rsqrt(square_d * inverse + EPS)
    scale_u = lax.rsqrt(square_u * inverse + EPS)
    down_lane = lane < R
    up_lane = jnp.logical_and(lane >= R, lane < 2 * R)
    low_lane = lane < 2 * R
    scale = jnp.where(down_lane, scale_d, scale_u)
    projected = jnp.where(low_lane, main, 0.0)
    pre = projected * scale
    sigma = jax.nn.sigmoid(pre)
    act = pre * sigma

    dg = pltpu.roll(main, 2 * R, axis=1)
    columns = []
    if ends:
        act_e = jnp.where(is_first, act[:, R : 2 * R], act[:, 0:R])
        cot_e = jnp.where(is_first, main[:, 3 * R :], main[:, 2 * R : 3 * R])
        own = jnp.concatenate([folded[:, R * r : R * r + R] for r in range(4)], axis=0)
        act_own = nn(act_e, own, HIGH)
        out_b = cot_e + act_own
        square_e = jnp.where(is_first, square_u, square_d)
        square_e = square_e + jnp.sum(act_e * (cot_e + out_b), axis=1, keepdims=True)
        scale_e = lax.rsqrt(jnp.maximum(square_e, 0.0) * inverse + EPS)
        cross = total[CROSS:ROWS]
        raw = total[PLAIN:CROSS] + nn(act_e, cross, HIGH)
        logits = raw * scale_e
        block = lax.div(place, LANES // PER)
        ids_d = down_ids[pl.ds(block, 1), :]
        ids_u = up_ids[pl.ds(block, 1), :]
        ids = jnp.where(is_first, ids_u, ids_d).astype(F32)
        group = lax.div(lane, R)
        within = lax.rem(lane, R)
        weight_sum = jnp.float32(0.0)
        for k in range(heads):
            weight_sum = weight_sum + loss_weights[k].astype(F32)
        top = jnp.zeros((PER, LANES), F32)
        target = jnp.zeros((PER, LANES), F32)
        weight = jnp.zeros((PER, LANES), F32)
        for k in range(heads):
            mine = group == k
            shift = offsets[k]
            largest = jnp.max(jnp.where(mine, logits, -jnp.inf), axis=1, keepdims=True)
            wanted = jnp.sum(jnp.where(lane == base + token + shift, ids, 0.0), axis=1, keepdims=True)
            factor = loss_weights[k].astype(F32) / weight_sum / ((M - shift) * sequences).astype(F32)
            valid = jnp.where(spot + shift < M, factor, 0.0)
            top = jnp.where(mine, largest, top)
            target = jnp.where(mine, wanted, target)
            weight = jnp.where(mine, valid, weight)
        power = jnp.exp(logits - top)
        below = jnp.ones((PER, LANES), F32)
        for k in range(heads):
            mine = group == k
            below = jnp.where(mine, jnp.sum(jnp.where(mine, power, 0.0), axis=1, keepdims=True), below)
        hit = jnp.where(within == target.astype(jnp.int32), 1.0, 0.0)
        per_lane = hit * (top + jnp.log(below) - logits) * weight
        loss = jnp.sum(jnp.sum(per_lane, axis=1, keepdims=True), axis=0, keepdims=True)
        grad = weight * (power / below - hit)
        grad_cols = grad * scale_e
        coef_e = jnp.sum(grad * raw, axis=1, keepdims=True) * scale_e * scale_e * scale_e * inverse
        dg_e = nt(grad_cols, cross, HIGH) - coef_e * out_b
        dg_wide = jnp.concatenate([dg_e] * 4, axis=1)
        replace = jnp.logical_or(jnp.logical_and(is_last, down_lane), jnp.logical_and(is_first, up_lane))
        dg = jnp.where(replace, dg_wide, dg)
        columns = [coef_e]
    d_pre = jnp.where(low_lane, dg * sigma * (1.0 + pre * (1.0 - sigma)), 0.0)
    d_scaled = d_pre * scale
    moved = d_pre * projected
    coef_d = jnp.sum(jnp.where(down_lane, moved, 0.0), axis=1, keepdims=True)
    coef_u = jnp.sum(jnp.where(up_lane, moved, 0.0), axis=1, keepdims=True)
    coef_d = coef_d * scale_d * scale_d * scale_d * inverse
    coef_u = coef_u * scale_u * scale_u * scale_u * inverse
    both = jnp.where(low_lane, act, pltpu.roll(d_scaled, 2 * R, axis=1))

    def parts_of(row):
        high = row.astype(BF16).astype(F32)
        low = (row - high).astype(BF16).astype(F32)
        return [high, low, row - high - low]

    rows = []
    for col in (coef_d, coef_u, *columns):
        row = jnp.sum(jnp.where(lane == token, col, 0.0), axis=0, keepdims=True)
        rows += parts_of(row)[0:2]
    if ends:
        rows += parts_of(jnp.broadcast_to(loss, (1, LANES)))
    rows += [jnp.zeros((16 - len(rows), LANES), F32)]
    chunk = jnp.concatenate([both] + rows + ([grad_cols] if ends else []), axis=0)
    out[...] = jnp.broadcast_to(chunk.astype(BF16)[None], out.shape)


def tokens_of(received, first):
    chunks = received.shape[0]
    return received[:, first : first + PER, :].reshape(chunks * PER, LANES)


def coefficient(received, row):
    chunks = received.shape[0]
    lane = lax.broadcasted_iota(jnp.int32, (PER, LANES), 1)
    token = lax.broadcasted_iota(jnp.int32, (PER, LANES), 0)
    cols = []
    for j in range(chunks):
        rows = received[j, PER:PLAIN, :].astype(F32)
        both = rows[row : row + 1] + rows[row + 1 : row + 2]
        cols.append(jnp.sum(jnp.where(lane == token, both, 0.0), axis=1, keepdims=True))
    return jnp.concatenate(cols, axis=0)


def at_rows(weights, group):
    zero = jnp.zeros_like(weights)
    return jnp.concatenate([weights if k == group else zero for k in range(LANES // R)], axis=0)


def backward(meta, received, x_d, x_u, c_d, c_u, w_d, w_u, gain, cand, outer, inner, g_d, g_u, loss, cot):
    is_first = meta[1] == 0
    is_last = meta[1] == meta[2] - 1
    is_even = lax.rem(meta[1], 2) == 0

    def fill(ahead, behind):
        act = tokens_of(received, 0)
        work = (
            (1, x_u, c_u, w_u, behind.at[0], ahead.at[1], g_u, is_first),
            (0, x_d, c_d, w_d, ahead.at[0], behind.at[1], g_d, is_last),
        )
        for side, x, c, w, y, dx, g, end in work:
            wide = x[...].astype(F32)
            y[...] = (wide + nn(act, at_rows(w[R : 2 * R], side))).astype(BF16)
            cot[...] = c[...].astype(F32)

            @pl.when(end)
            def _():
                high, low = halves(columns_of(gain, cand))
                grad = tokens_of(received, PLAIN)
                final = x[...].astype(F32) + nn(act, at_rows(w[R : 2 * R], side))
                cot[...] = nn(grad, high) + nn(grad, low) - coefficient(received, 4) * final

            held = cot[...]
            back = held + nn(act, at_rows(w[0:R], 2 + side)) - coefficient(received, 2 * side) * wide
            dx[...] = back.astype(BF16)
            by_cot = tn(act, held.astype(BF16))
            by_x = tn(act, x[...])
            grads = jnp.concatenate(
                [by_x[64 + R * side : 64 + R * side + R], by_cot[R * side : R * side + R]], axis=0
            )
            g[...] = grads.astype(g.dtype)

    @pl.when(is_even)
    def _():
        fill(inner, outer)

    @pl.when(jnp.logical_not(is_even))
    def _():
        fill(outer, inner)

    rows = jnp.sum(received[:, PER:PLAIN, :].astype(F32), axis=0)
    total = rows[6:7] + rows[7:8] + rows[8:9]
    loss[...] = jnp.broadcast_to(total, loss.shape)


def finish(
    meta, outer, inner, g_d, mate, losses, down_next, up_next, down_back, up_back, grad_a, grad_b, loss, sems
):
    is_even = lax.rem(meta[1], 2) == 0

    def copies_of(ahead, behind):
        return [
            pltpu.make_async_copy(ahead.at[0], down_next, sems.at[0]),
            pltpu.make_async_copy(behind.at[0], up_next, sems.at[1]),
            pltpu.make_async_copy(behind.at[1], down_back, sems.at[2]),
            pltpu.make_async_copy(ahead.at[1], up_back, sems.at[3]),
        ]

    @pl.when(is_even)
    def _():
        for copy in copies_of(outer, inner):
            copy.start()

    @pl.when(jnp.logical_not(is_even))
    def _():
        for copy in copies_of(inner, outer):
            copy.start()

    total = g_d[...] + mate[...].astype(F32)
    grad_a[...] = total[0:R]
    grad_b[...] = total[R : 2 * R]
    loss[0] = jnp.sum(losses[:, 0:1])

    @pl.when(is_even)
    def _():
        for copy in copies_of(outer, inner):
            copy.wait()

    @pl.when(jnp.logical_not(is_even))
    def _():
        for copy in copies_of(inner, outer):
            copy.wait()


def shards(
    down_in,
    up_in,
    down_cot,
    up_cot,
    adapt_a,
    adapt_b,
    head_gain,
    cand,
    down_ids,
    up_ids,
    offsets,
    loss_weights,
):
    sections = lax.axis_size("section")
    groups = lax.axis_size("dp")
    position = lax.axis_index("section")
    place = lax.axis_index("dp")
    tokens, local_width = down_in.shape[1:]
    heads, candidates = head_gain.shape[0], cand.shape[0]
    mirror = [(i, sections - 1 - i) for i in range(sections)]
    inside = [(i, i ^ 1) for i in range(sections)]
    between = [(i, i + 1 if i % 2 else i - 1) for i in range(1, sections - 1)]
    smem = pl.BlockSpec(memory_space=pltpu.SMEM)
    vmem = pl.BlockSpec(memory_space=pltpu.VMEM)
    hbm = pl.BlockSpec(memory_space=pltpu.HBM)
    params = pltpu.CompilerParams(vmem_limit_bytes=48 << 20)
    shape = jax.ShapeDtypeStruct
    wide = shape((tokens, local_width), BF16)
    both = shape((2, tokens, local_width), BF16)

    w_d = pl.pallas_call(
        packed,
        out_shape=shape((2 * R, local_width), BF16),
        in_specs=[hbm] * 2,
        out_specs=vmem,
        scratch_shapes=[pltpu.SemaphoreType.DMA((2,))],
        compiler_params=params,
    )(in_hbm(adapt_a[0].T), in_hbm(adapt_b[0]))
    w_u = lax.ppermute(w_d, "section", mirror)
    sizes = jnp.int32(sections), jnp.int32(head_gain.shape[1])
    meta = jnp.stack([place.astype(jnp.int32), position.astype(jnp.int32), *sizes])
    id_rows = (tokens // LANES, LANES)
    ids = down_ids.reshape(id_rows), up_ids.reshape(id_rows)
    fetched = (down_in[0], up_in[0], down_cot[0], up_cot[0], head_gain, cand, *ids, offsets, loss_weights)

    near = tokens // PER
    rings = [list(range(first, first + near)) for first in range(0, groups, near)]
    partners = [list(members) for members in zip(*rings)]
    send = shape((near, ROWS, LANES), BF16)
    partial, x_d, x_u, c_d, c_u, gain_part, cand_part, ids_d, ids_u, shifts, shares = pl.pallas_call(
        first_partial,
        out_shape=(
            send,
            wide,
            wide,
            wide,
            wide,
            shape((heads, local_width), F32),
            shape((candidates, local_width), BF16),
            shape(id_rows, jnp.int32),
            shape(id_rows, jnp.int32),
            shape(offsets.shape, jnp.int32),
            shape(loss_weights.shape, jnp.int32),
        ),
        in_specs=[smem] + [hbm] * 10 + [vmem],
        out_specs=(vmem,) * 9 + (smem,) * 2,
        scratch_shapes=[pltpu.SemaphoreType.DMA((10,))],
        compiler_params=params,
    )(meta, *(in_hbm(held) for held in fetched), w_d)

    def over_dp(rows, back_rows):
        def run(meta, partial, x_u, c_u, w_d, w_u, gain_part, cand_part, shifts, shares, ids_d, ids_u):
            chunk = pl.pallas_call(
                second_partial,
                out_shape=shape((near, rows, LANES), BF16),
                in_specs=[smem] + [vmem] * 7,
                out_specs=vmem,
                compiler_params=params,
            )(meta, partial, x_u, c_u, w_u, w_d, gain_part, cand_part)
            received = lax.all_to_all(chunk, "dp", 0, 0, axis_index_groups=rings)
            summed = pl.pallas_call(
                gathered_sum,
                out_shape=shape((rows, LANES), BF16),
                in_specs=[vmem],
                out_specs=vmem,
                compiler_params=params,
            )(received)
            received = lax.all_gather(summed, "dp", axis_index_groups=partners)
            back = pl.pallas_call(
                middle,
                out_shape=shape((near, back_rows, LANES), BF16),
                in_specs=[smem] * 3 + [vmem] * 3,
                out_specs=vmem,
                compiler_params=params,
            )(meta, shifts, shares, received, ids_d, ids_u)
            gathered = lax.all_to_all(back, "dp", 0, 0, axis_index_groups=rings)
            return jnp.pad(gathered, ((0, 0), (0, BACK_ROWS - back_rows), (0, 0)))

        return run

    held = (meta, partial, x_u, c_u, w_d, w_u, gain_part, cand_part, shifts, shares, ids_d, ids_u)
    is_end = jnp.logical_or(position == 0, position == sections - 1)
    gathered = lax.cond(is_end, over_dp(ROWS, BACK_ROWS), over_dp(PLAIN, PLAIN), *held)
    outer, inner, g_d, g_u, loss_rows = pl.pallas_call(
        backward,
        out_shape=(
            both,
            both,
            shape((2 * R, local_width), F32),
            shape((2 * R, local_width), BF16),
            shape((sections, LANES), F32),
        ),
        in_specs=[smem] + [vmem] * 9,
        out_specs=(vmem,) * 5,
        scratch_shapes=[pltpu.VMEM((tokens, local_width), F32)],
        compiler_params=params,
    )(meta, gathered, x_d, x_u, c_d, c_u, w_d, w_u, gain_part, cand_part)
    outer = lax.ppermute(outer, "section", between)
    inner = lax.ppermute(inner, "section", inside)
    mate = lax.ppermute(g_u, "section", mirror)
    losses = lax.all_to_all(loss_rows, "section", 0, 0, tiled=True)
    down_next, up_next, down_back, up_back, grad_a, grad_b, loss = pl.pallas_call(
        finish,
        out_shape=(
            wide,
            wide,
            wide,
            wide,
            shape((R, local_width), F32),
            shape((R, local_width), F32),
            shape((1,), F32),
        ),
        in_specs=[smem] + [vmem] * 5,
        out_specs=(hbm,) * 4 + (vmem, vmem, smem),
        scratch_shapes=[pltpu.SemaphoreType.DMA((4,))],
        compiler_params=params,
    )(meta, outer, inner, g_d, mate, losses)
    return (
        down_next[None],
        up_next[None],
        down_back[None],
        up_back[None],
        grad_a.T[None],
        grad_b[None],
        loss,
    )


def solution(mesh):
    in_specs = (
        P("section", None, "dp"),
        P("section", None, "dp"),
        P("section", None, "dp"),
        P("section", None, "dp"),
        P("section", "dp", None),
        P("section", None, "dp"),
        P(),
        P(),
        P(),
        P(),
        P(),
        P(),
    )
    out_specs = (
        P("section", None, "dp"),
        P("section", None, "dp"),
        P("section", None, "dp"),
        P("section", None, "dp"),
        P("section", "dp", None),
        P("section", None, "dp"),
        P(),
    )
    return jax.shard_map(shards, mesh=mesh, in_specs=in_specs, out_specs=out_specs, check_vma=False)
```
